512 devices in a mesh: grp: 8 (over x, core), seg: 64 (over z, y).
Axes of the slice: x: 4, y: 8, z: 8, core: 2. Of those that a mesh axis runs over, the one named last changes fastest.
Arguments:
- positions: float32 [3, 2097152], P(None, ('grp', 'seg')), may hold values from -18 to 18
- normals: float32 [3, 2097152], P(None, ('grp', 'seg')), may hold values from -3 to 3
- scales: float32 [2097152], P(('grp', 'seg')), may hold values from 0.5 to 2
- displacement: float32 [3, 2097152], P(None, ('grp', 'seg')), may hold values from -6 to 6
- pair_list: int32 [2, 81920], P(None, ('grp', 'seg')), may hold values from 0 to 63, as said below
- pair_count: int32 [512], P(('grp', 'seg')), may hold values from 32 to 160, as said below
- base_aperture: float32 [2097152], P(('grp', 'seg')), may hold values from 0.5 to 1.2
- storage: float32 [2097152], P(('grp', 'seg')), may hold values from 0.5 to 2
- injection: float32 [2097152], P(('grp', 'seg')), may hold values from -6 to 6
- link_offset: int32 [2097152], P(('grp', 'seg')), may hold values from 1 to 4096
Outputs:
- traction: float32 [3, 2097152], P(None, ('grp', 'seg'))
- pressure: float32 [2097152], P(('grp', 'seg'))
- residual: float32 [2097152], P(('grp', 'seg'))
The draws below stay inside these ranges and needn't reach their ends.
Inputs may be any that keep to these rules, and one draw needn't show every extreme that they name: `pair_list`: in each device's 160 slots, the first 32 pairs are (t, t + 32) for t = 0 to 31; every other used pair (t, s) has t + 1 <= s + 1 <= t + 32, i.e. s from t to t + 31; no used pair occurs twice; slots from pair_count on hold (0, 32) and are unused. `pair_count`: some device uses all 160 slots.
All inputs are finite; a program needn't handle non-finite values.
Results may differ from the reference program's by a relative error of at most 0.0003.
Values sent between devices are 32-bit elements; how exact they have to be, the bound alone decides.
A program may use at most 64 MiB of HBM per device.

```python
import math
import jax
import jax.numpy as jnp
from jax import lax

E_DEV = 4096
BLK = 128
ITERS = 2
NB = 32
PMAX = 160
ELEMS = 2097152
DEVICES = 512


def pair_tables(key):
    key_count, key_busy, key_pick = jax.random.split(key, 3)
    spread = jax.random.randint(key_count, (DEVICES,), 0, 65)
    extra = (PMAX - NB) * spread * spread // 4096
    busy = jax.random.randint(key_busy, (), 0, DEVICES)
    extra = jnp.where(jnp.arange(DEVICES) == busy, PMAX - NB, extra)
    count = (NB + extra).astype(jnp.int32)
    keys = jax.random.split(key_pick, DEVICES)
    chosen = jax.vmap(lambda k: jax.random.permutation(k, NB * NB)[:PMAX - NB])(keys).astype(jnp.int32)
    t_off = chosen // NB
    s_off = t_off + chosen % NB
    diag = jnp.broadcast_to(jnp.arange(NB, dtype=jnp.int32), (DEVICES, NB))
    target = jnp.concatenate([diag, t_off], 1)
    source = jnp.concatenate([diag + NB, s_off], 1)
    used = jnp.arange(PMAX, dtype=jnp.int32)[None, :] < count[:, None]
    target = jnp.where(used, target, 0)
    source = jnp.where(used, source, NB)
    return (jnp.stack([target.reshape(-1), source.reshape(-1)]).astype(jnp.int32), count)


def draw_pair_list(key, part):
    return pair_tables(key)[0]


def draw_pair_count(key, part):
    return pair_tables(key)[1]


def touch_ends(entries, rng, smallest, high):
    spot = [jax.random.randint(jax.random.fold_in(rng, axis), (), 0, length) for axis, length in enumerate(entries.shape)]
    longest = entries.shape.index(max(entries.shape))
    neighbour = spot[:longest] + [(spot[longest] + 1) % entries.shape[longest]] + spot[longest + 1:]
    return entries.at[tuple(spot)].set(smallest).at[tuple(neighbour)].set(high)


def level_of(key, extent, cuts, smallest, largest):
    level = 1.0
    for dim, parts in cuts:
        steps = jax.random.uniform(jax.random.fold_in(jax.random.fold_in(key, 6), dim), (parts,), jnp.float32, smallest / len(cuts), largest / len(cuts))
        level = level * jnp.repeat(jnp.exp(steps), extent[dim] // parts).reshape((-1,) + (1,) * (len(extent) - 1 - dim))
    return level


def normal_values(rng, shape, scale, most, shards=(), held_as=jnp.bfloat16):
    loudness = level_of(rng, shape, shards, -0.22, 0.18) if shards else 1.0
    values = jax.random.normal(rng, shape, jnp.float32) * scale * loudness
    return jnp.minimum(jnp.maximum(values, -most), most).astype(held_as)


def setup_inputs(seed: int = 0) -> dict:
    key_list = jax.random.split(jax.random.key(seed), 11)
    positions = normal_values(key_list[0], (3, ELEMS), 3.0, 18.0, ((1, 512),), jnp.float32)
    normals = normal_values(key_list[1], (3, ELEMS), 0.577, 3.0, ((1, 512),), jnp.float32)
    scales = jnp.clip(jnp.exp(math.log(2.0) - 1.3862944 * jax.random.uniform(key_list[2], (ELEMS,), jnp.float32) ** level_of(key_list[2], (ELEMS,), ((0, 512),), -0.2, 0.2)), 0.5, 2.0)
    displacement = normal_values(key_list[3], (3, ELEMS), 1.0, 6.0, ((1, 512),), jnp.float32)
    pair_list = draw_pair_list(jax.random.fold_in(key_list[10], 71), 0)
    pair_count = draw_pair_count(jax.random.fold_in(key_list[10], 71), 0)
    base_aperture = jnp.clip(jnp.exp(math.log(1.2) - 0.8754688 * jax.random.uniform(key_list[6], (ELEMS,), jnp.float32) ** level_of(key_list[6], (ELEMS,), ((0, 512),), -0.2, 0.2)), 0.5, 1.2)
    storage = jnp.clip(0.5 + 1.5 * jax.random.uniform(key_list[7], (ELEMS,), jnp.float32) ** level_of(key_list[7], (ELEMS,), ((0, 512),), -0.2, 0.2), 0.5, 2.0)
    injection = normal_values(key_list[8], (ELEMS,), 1.0, 6.0, ((0, 512),), jnp.float32)
    link_offset = touch_ends(jax.random.randint(key_list[9], (ELEMS,), 1, E_DEV + 1), jax.random.fold_in(key_list[9], 1), 1, E_DEV).astype(jnp.int32)
    return {"positions": positions, "normals": normals, "scales": scales, "displacement": displacement, "pair_list": pair_list, "pair_count": pair_count, "base_aperture": base_aperture, "storage": storage, "injection": injection, "link_offset": link_offset}


def tiles(tpos, tnrm, tscl, spos, snrm, sscl):
    dist = jnp.zeros(tscl.shape + (sscl.shape[-1],), jnp.float32)
    align = jnp.zeros(tscl.shape + (sscl.shape[-1],), jnp.float32)
    for comp in range(3):
        diff = tpos[comp][:, :, None] - spos[comp][:, None, :]
        dist = dist + diff * diff
        align = align + tnrm[comp][:, :, None] * snrm[comp][:, None, :]
    return 0.25 * tscl[:, :, None] * sscl[:, None, :] * (1.0 + 0.5 * align) / jnp.sqrt(0.25 + dist)

def flow_apply(vec, weight, target, storage):
    flux = weight * (vec - vec[target])
    return storage * vec + flux + jnp.zeros_like(vec).at[target].add(-flux)

def reference(positions, normals, scales, displacement, pair_list, pair_count, base_aperture, storage, injection, link_offset):
    total = positions.shape[1]
    front = NB * BLK
    pos_pad = jnp.concatenate([jnp.zeros((3, front), jnp.float32), positions], 1).reshape(3, -1, BLK)
    nrm_pad = jnp.concatenate([jnp.zeros((3, front), jnp.float32), normals], 1).reshape(3, -1, BLK)
    scl_pad = jnp.concatenate([jnp.zeros((front,), jnp.float32), scales], 0).reshape(-1, BLK)
    dsp_pad = jnp.concatenate([jnp.zeros((3, front), jnp.float32), displacement], 1).reshape(3, -1, BLK)
    npairs = pair_list.shape[1]
    index = jnp.arange(npairs, dtype=jnp.int32)
    device = index // PMAX
    slot = index % PMAX
    valid = (slot < pair_count[device]).astype(jnp.float32)
    target = device * NB + pair_list[0] + NB
    source = device * NB + pair_list[1]
    mirrored = valid * (source != target).astype(jnp.float32)
    group = math.gcd(npairs, 64)
    packed = (target.reshape(-1, group), source.reshape(-1, group), valid.reshape(-1, group), mirrored.reshape(-1, group))

    def step(acc, item):
        tgt, src, wf, wb = item
        kern = tiles(pos_pad[:, tgt], nrm_pad[:, tgt], scl_pad[tgt], pos_pad[:, src], nrm_pad[:, src], scl_pad[src])
        fwd = jnp.einsum('gab,cgb->cga', kern, dsp_pad[:, src], precision=lax.Precision.HIGHEST) * wf[None, :, None]
        bck = jnp.einsum('gab,cga->cgb', kern, dsp_pad[:, tgt], precision=lax.Precision.HIGHEST) * wb[None, :, None]
        return (acc.at[:, tgt].add(fwd).at[:, src].add(bck), None)
    acc, _ = lax.scan(step, jnp.zeros(dsp_pad.shape, jnp.float32), packed)
    traction = acc[:, NB:].reshape(3, total)
    aperture = base_aperture * (1.0 + 0.5 * jnp.tanh(traction[0]))
    cube = aperture * aperture * aperture
    far = jnp.arange(total, dtype=jnp.int32) + link_offset
    inside = (far < total).astype(jnp.float32)
    target_el = jnp.minimum(far, total - 1).astype(jnp.int32)
    weight = 0.5 * (cube + cube[target_el]) * inside
    pressure = jnp.zeros_like(injection)
    residual, direction = (injection, injection)
    norm_now = jnp.sum(residual * residual)
    for it in range(ITERS):
        image = flow_apply(direction, weight, target_el, storage)
        alpha = norm_now / jnp.sum(direction * image)
        pressure = pressure + alpha * direction
        residual = residual - alpha * image
        norm_next = jnp.sum(residual * residual)
        direction = residual + norm_next / norm_now * direction
        norm_now = norm_next
    return (traction, pressure, residual)
```

```python
import functools

import jax
import jax.numpy as jnp
from jax import lax
from jax.experimental import pallas as pl
from jax.experimental.pallas import tpu as pltpu
from jax.sharding import PartitionSpec as P

BLK = 128
NB = 32
PMAX = 160
F32 = jnp.float32
BF16 = jnp.bfloat16
MESH = pl.DeviceIdType.MESH
NT = (((1,), (1,)), ((), ()))
UNROLL = 8


def split(x, parts):
    out = []
    for _ in range(parts - 1):
        top = x.astype(BF16).astype(F32)
        out.append(top)
        x = x - top
    return out + [x]


def quads(vec, last):
    return jnp.concatenate([vec, last, vec, last], 0)


def kernel(
    grp_size,
    seg_size,
    low_size,
    pairs,
    count,
    pos,
    nrm,
    scl,
    dsp,
    pair_rows,
    base,
    sto,
    inj,
    off,
    traction,
    pressure,
    residual,
    prev_pos,
    prev_nrm,
    prev_scl,
    prev_dsp,
    base_next,
    table_inj,
    tfeat,
    sfeat,
    dfeat,
    held,
    con_t,
    con_s,
    near0,
    near12,
    got0,
    got0_far,
    got12,
    onehot,
    lanes_hot,
    rows_hot,
    spread,
    table,
    landed_out,
    landed_in,
    part_out,
    part_in,
    landed2_out,
    landed2_in,
    sums_out,
    sums_grp,
    sums_low,
    sums_high,
    send_sem,
    recv_sem,
    red_send,
    red_recv,
):
    devices = grp_size * seg_size
    high_size = seg_size // low_size
    grp = lax.axis_index("grp")
    seg = lax.axis_index("seg")
    me = grp * seg_size + seg

    def device(shift):
        to = lax.rem(me + shift + devices, devices)
        return (to // seg_size, lax.rem(to, seg_size))

    def grp_mate(j):
        return (lax.rem(grp + j, grp_size), seg)

    def low_mate(j):
        return (grp, seg // low_size * low_size + lax.rem(lax.rem(seg, low_size) + j, low_size))

    def high_mate(j):
        return (grp, lax.rem(seg + j * low_size, seg_size))

    mates = [device(shift) for shift in (1, -1, 2, -2)]
    mates += [grp_mate(j) for j in range(1, grp_size)]
    mates += [low_mate(j) for j in range(1, low_size)]
    mates += [high_mate(j) for j in range(1, high_size)]
    barrier = pltpu.get_barrier_semaphore()
    for mate in mates:
        pl.semaphore_signal(barrier, inc=1, device_id=mate, device_id_type=MESH)
    pl.semaphore_wait(barrier, len(mates))

    def send(src, dst, slot, to):
        copy = pltpu.make_async_remote_copy(
            src_ref=src,
            dst_ref=dst,
            send_sem=send_sem.at[slot],
            recv_sem=recv_sem.at[slot],
            device_id=to,
            device_id_type=MESH,
        )
        copy.start()
        return copy

    after, before, before2 = device(1), device(-1), device(-2)
    frame = [
        send(pos, prev_pos, 0, after),
        send(nrm, prev_nrm, 1, after),
        send(scl, prev_scl, 2, after),
        send(dsp, prev_dsp, 3, after),
    ]
    early = [
        send(base, base_next, 4, before),
        send(inj, table_inj.at[pl.ds(NB, NB)], 5, before),
    ]

    row = lax.broadcasted_iota(jnp.int32, (8, BLK), 0)
    low4 = row < 4
    is3 = row == 3
    is7 = row == 7
    is_norm = is3 | is7
    zeros8 = jnp.zeros((8, BLK), F32)
    centre = jnp.mean(pos[...], axis=1, keepdims=True)

    def target_block(k, _):
        lane = pl.ds(pl.multiple_of(k * BLK, BLK), BLK)
        p = pos[:, lane] - centre
        q = quads(p, jnp.sum(p * p, axis=0, keepdims=True))
        q1, q2, q3 = split(jnp.where(is_norm, q, -2.0 * q), 3)
        s = scl[pl.ds(k, 1), :]
        r = quads(nrm[:, lane] * s * 0.125, 0.25 * s)
        r1, r2, r3 = split(r, 3)
        rows = [
            jnp.where(is7, 1.0, q1),
            jnp.where(is7, 1.0, q2),
            jnp.where(is7, 1.0, jnp.where(low4, q3, q1)),
            r1,
            r2,
            jnp.where(low4, r3, r1),
        ]
        rows += [zeros8] * 10
        tfeat[k] = jnp.concatenate(rows, 0).T[:, :48].astype(BF16)
        return 0

    def source_block(pos_ref, nrm_ref, scl_ref, dsp_ref, first, factor, k, _):
        lane = pl.ds(pl.multiple_of(k * BLK, BLK), BLK)
        p = pos_ref[:, lane] - centre
        q1, q2, q3 = split(quads(p, jnp.sum(p * p, axis=0, keepdims=True) + 0.25), 3)
        s = scl_ref[pl.ds(k, 1), :]
        if factor is not None:
            s = jnp.where(factor, s, 0.0)
        r1, r2, r3 = split(quads(nrm_ref[:, lane] * s, s), 3)
        ahead = [
            jnp.where(is3, 1.0, jnp.where(is7 | low4, q1, q2)),
            jnp.where(is3, 1.0, jnp.where(low4, q1, q2)),
            jnp.where(is3, 1.0, jnp.where(low4, q1, q3)),
            zeros8,
            zeros8,
            zeros8,
        ]
        align = [
            zeros8,
            zeros8,
            zeros8,
            jnp.where(low4, r1, r2),
            jnp.where(low4, r1, r2),
            jnp.where(low4, r1, r3),
        ]
        sfeat[first + k, :, :BLK] = jnp.concatenate(ahead, 0).astype(BF16)
        sfeat[first + k, :, BLK:] = jnp.concatenate(align, 0).astype(BF16)
        d = dsp_ref[:, lane]
        d1, d2 = split(quads(d, jnp.zeros((1, BLK), F32)), 2)
        both = jnp.concatenate([jnp.where(low4, d1, d2), zeros8], 0).astype(BF16)
        dfeat[first + k, :, :BLK] = both
        dfeat[first + k, :, BLK:] = both
        return 0

    lax.fori_loop(0, NB, target_block, 0)
    lax.fori_loop(0, NB, functools.partial(source_block, pos, nrm, scl, dsp, NB, None), 0)

    slot = lax.broadcasted_iota(jnp.int32, (2 * NB, PMAX), 1)
    block = lax.broadcasted_iota(jnp.int32, (2 * NB, PMAX), 0)
    tgt = pair_rows[0:1, :] + NB
    src = pair_rows[1:2, :]
    live = slot < count[0]
    onehot[0] = jnp.where(live & (block == tgt), 1.0, 0.0).astype(BF16)
    onehot[1] = jnp.where(live & (block == src) & (src != tgt), 1.0, 0.0).astype(BF16)

    element = (
        lax.broadcasted_iota(jnp.int32, (NB, BLK), 0) * BLK
        + lax.broadcasted_iota(jnp.int32, (NB, BLK), 1)
    )
    partner = element + off[...]
    part_row = partner >> 7
    part_lane = partner & 127
    inside = jnp.where((me < devices - 1) | (partner < NB * BLK), 0.5, 0.0).astype(F32)
    iota_lane = lax.broadcasted_iota(jnp.int32, (BLK, BLK), 0)
    iota_row = lax.broadcasted_iota(jnp.int32, (2 * NB, BLK), 0)
    for k in range(NB):
        lane = pl.ds(k * BLK, BLK)
        lanes_hot[:, lane] = jnp.where(iota_lane == part_lane[k : k + 1], 1.0, 0.0).astype(BF16)
        rows_hot[:, lane] = jnp.where(iota_row == part_row[k : k + 1], 1.0, 0.0).astype(BF16)

    def gather(ref):
        out = []
        for v in range(NB // 8):
            lane = part_lane[8 * v : 8 * v + 8]
            hot = part_row[8 * v : 8 * v + 8]
            acc = jnp.zeros((8, BLK), F32)
            for h in range(8 * v, 8 * v + 8 + NB):
                line = jnp.broadcast_to(ref[h : h + 1, :], (8, BLK))
                got = jnp.take_along_axis(line, lane, axis=1, mode="promise_in_bounds")
                acc = jnp.where(hot == h, got, acc)
            out.append(acc)
        return jnp.concatenate(out, 0)

    def scatter(flux):
        top = flux.astype(BF16)
        rest = (flux - top.astype(F32)).astype(BF16)
        for k in range(NB):
            lane = pl.ds(k * BLK, BLK)
            hot = rows_hot[:, lane]
            spread[: 2 * NB, lane] = hot * top[k : k + 1]
            spread[2 * NB :, lane] = hot * rest[k : k + 1]
        both = lax.dot_general(spread[...], lanes_hot[...], NT, preferred_element_type=F32)
        return both[: 2 * NB] + both[2 * NB :]

    vec = inj[...]
    table_inj[:NB, :] = vec
    for copy in early:
        copy.wait_recv()
    vec_diff = vec - gather(table_inj)

    def apply(p, u):
        t = pairs[0, p] + NB
        s = pairs[1, p]
        hl = held[u]
        con_t[p] = lax.dot_general(dfeat[s], hl, NT, preferred_element_type=F32)[:8]
        back = jnp.dot(dfeat[t, :, :BLK], hl, preferred_element_type=F32)[:8]
        con_s[p] = back[:, :BLK] + back[:, BLK:]

    def evaluate(p, u):
        m = jnp.dot(tfeat[pairs[0, p]], sfeat[pairs[1, p]], preferred_element_type=F32)
        g = m[:, BLK:] * lax.rsqrt(m[:, :BLK])
        top = g.astype(BF16)
        held[u, :, :BLK] = top
        held[u, :, BLK:] = (g - top.astype(F32)).astype(BF16)

    def steps(i, _):
        for u in range(UNROLL):
            apply((i - 1) * UNROLL + u, u)
            evaluate(i * UNROLL + u, u)
        return 0

    for u in range(UNROLL):
        evaluate(u, u)
    lax.fori_loop(1, NB // UNROLL, steps, 0)
    for copy in frame:
        copy.wait_recv()
    lax.fori_loop(
        0, NB, functools.partial(source_block, prev_pos, prev_nrm, prev_scl, prev_dsp, 0, me > 0), 0
    )
    lax.fori_loop(NB // UNROLL, PMAX // UNROLL, steps, 0)
    for u in range(UNROLL):
        apply(PMAX - UNROLL + u, u)

    def component(c):
        def lines(ref):
            x = ref[:, c, :] + ref[:, c + 4, :]
            top = x.astype(BF16)
            return top, (x - top.astype(F32)).astype(BF16)

        out = jnp.zeros((2 * NB, BLK), F32)
        for which, ref in ((0, con_t), (1, con_s)):
            hot = onehot[which]
            for x in lines(ref):
                out = out + jnp.dot(hot, x, preferred_element_type=F32)
        return out

    first = component(0)
    near0[...] = first
    move0 = [send(near0, got0, 6, before), send(near0.at[pl.ds(0, NB)], got0_far, 7, before2)]
    second, third = component(1), component(2)
    near12[0] = second[:NB]
    near12[1] = third[:NB]
    move12 = send(near12, got12, 8, before)

    def cubed(scale, t):
        aperture = scale * (1.0 + 0.5 * jnp.tanh(t))
        return aperture * aperture * aperture

    for copy in move0:
        copy.wait_recv()
    traction0 = first[NB:] + got0[:NB, :]
    cube = cubed(base[...], traction0)
    table[:NB, :] = cube
    table[NB:, :] = cubed(base_next[...], got0[NB:, :] + got0_far[...])
    weight = inside * (cube + gather(table))

    flux = weight * vec_diff
    landed = scatter(flux)
    part = sto[...] * vec + flux - landed[:NB]
    landed_out[...] = landed[NB:]
    part_out[...] = part
    move_q = [send(landed_out, landed_in, 9, after), send(part_out, part_in, 10, before)]
    for copy in move_q:
        copy.wait_recv()
    q = part - landed_in[...]
    table[:NB, :] = q
    table[NB:, :] = part_in[...] - landed[NB:]
    q_diff = q - gather(table)
    flux = weight * q_diff

    def line(x):
        return jnp.sum(x, axis=0, keepdims=True)

    rows = [line(vec * vec), line(vec * q), line(q * q), line(sto[...] * q * q + flux * q_diff)]
    sums = jnp.concatenate(rows + [jnp.zeros((4, BLK), F32)], 0)

    def exchange(stage, sums, size, mate, got):
        if size == 1:
            return sums
        sums_out[stage] = sums
        for j in range(1, size):
            pltpu.make_async_remote_copy(
                src_ref=sums_out.at[stage],
                dst_ref=got.at[j - 1],
                send_sem=red_send.at[stage],
                recv_sem=red_recv.at[stage],
                device_id=mate(j),
                device_id_type=MESH,
            ).start()

    def collect(stage, sums, size, got):
        if size == 1:
            return sums
        pltpu.make_async_copy(got, got, red_recv.at[stage]).wait()
        for j in range(size - 1):
            sums = sums + got[j]
        return sums

    exchange(0, sums, grp_size, grp_mate, sums_grp)
    landed = scatter(flux)
    landed2_out[...] = landed[NB:]
    move_u = send(landed2_out, landed2_in, 11, after)
    u_part = sto[...] * q + flux - landed[:NB]
    sums = collect(0, sums, grp_size, sums_grp)
    exchange(1, sums, low_size, low_mate, sums_low)
    move12.wait_recv()
    full = [traction0, second[NB:] + got12[0], third[NB:] + got12[1]]
    for k in range(NB):
        rows = [x[k : k + 1] for x in full]
        traction[:, pl.ds(k * BLK, BLK)] = jnp.concatenate(rows, 0)
    sums = collect(1, sums, low_size, sums_low)
    exchange(2, sums, high_size, high_mate, sums_high)
    move_u.wait_recv()
    u = u_part - landed2_in[...]
    sums = collect(2, sums, high_size, sums_high)

    total = jnp.sum(sums, axis=1, keepdims=True)
    rr0, r0q, qq, qu = (total[j : j + 1] for j in range(4))
    alpha0 = rr0 / r0q
    rr1 = alpha0 * alpha0 * qq - rr0
    beta = rr1 / rr0
    alpha1 = rr1 / (r0q - 2.0 * alpha0 * qq + alpha0 * alpha0 * qu - beta * rr1 / alpha0)
    keep = 1.0 + beta
    r1 = vec - alpha0 * q
    residual[...] = r1 - alpha1 * (keep * q - alpha0 * u)
    pressure[...] = alpha0 * vec + alpha1 * (r1 + beta * vec)

    for copy in frame + early + move0 + [move12] + move_q + [move_u]:
        copy.wait_send()
    for stage, (size, got) in enumerate(
        ((grp_size, sums_grp), (low_size, sums_low), (high_size, sums_high))
    ):
        if size > 1:
            pltpu.make_async_copy(got, got, red_send.at[stage]).wait()


def shards(
    grp_size,
    seg_size,
    positions,
    normals,
    scales,
    displacement,
    pair_list,
    pair_count,
    base_aperture,
    storage,
    injection,
    link_offset,
):
    low_size = 8 if seg_size % 8 == 0 else 2
    high_size = seg_size // low_size
    square = (NB, BLK)
    vmem = pl.BlockSpec(memory_space=pltpu.VMEM)
    smem = pl.BlockSpec(memory_space=pltpu.SMEM)
    scratch = [
        pltpu.VMEM((3, NB * BLK), F32),
        pltpu.VMEM((3, NB * BLK), F32),
        pltpu.VMEM(square, F32),
        pltpu.VMEM((3, NB * BLK), F32),
        pltpu.VMEM(square, F32),
        pltpu.VMEM((2 * NB, BLK), F32),
        pltpu.VMEM((NB, BLK, 48), BF16),
        pltpu.VMEM((2 * NB, 48, 2 * BLK), BF16),
        pltpu.VMEM((2 * NB, 16, 2 * BLK), BF16),
        pltpu.VMEM((UNROLL, BLK, 2 * BLK), BF16),
        pltpu.VMEM((PMAX, 8, BLK), F32),
        pltpu.VMEM((PMAX, 8, BLK), F32),
        pltpu.VMEM((2 * NB, BLK), F32),
        pltpu.VMEM((2, NB, BLK), F32),
        pltpu.VMEM((2 * NB, BLK), F32),
        pltpu.VMEM(square, F32),
        pltpu.VMEM((2, NB, BLK), F32),
        pltpu.VMEM((2, 2 * NB, PMAX), BF16),
        pltpu.VMEM((BLK, NB * BLK), BF16),
        pltpu.VMEM((2 * NB, NB * BLK), BF16),
        pltpu.VMEM((4 * NB, NB * BLK), BF16),
        pltpu.VMEM((2 * NB, BLK), F32),
        pltpu.VMEM(square, F32),
        pltpu.VMEM(square, F32),
        pltpu.VMEM(square, F32),
        pltpu.VMEM(square, F32),
        pltpu.VMEM(square, F32),
        pltpu.VMEM(square, F32),
        pltpu.VMEM((3, 8, BLK), F32),
        pltpu.VMEM((max(grp_size - 1, 1), 8, BLK), F32),
        pltpu.VMEM((max(low_size - 1, 1), 8, BLK), F32),
        pltpu.VMEM((max(high_size - 1, 1), 8, BLK), F32),
        pltpu.SemaphoreType.DMA((12,)),
        pltpu.SemaphoreType.DMA((12,)),
        pltpu.SemaphoreType.DMA((3,)),
        pltpu.SemaphoreType.DMA((3,)),
    ]
    traction, pressure, residual = pl.pallas_call(
        functools.partial(kernel, grp_size, seg_size, low_size),
        out_shape=(
            jax.ShapeDtypeStruct((3, NB * BLK), F32),
            jax.ShapeDtypeStruct(square, F32),
            jax.ShapeDtypeStruct(square, F32),
        ),
        in_specs=[smem, smem] + [vmem] * 9,
        out_specs=(vmem, vmem, vmem),
        scratch_shapes=scratch,
        compiler_params=pltpu.CompilerParams(
            collective_id=0, has_side_effects=True, vmem_limit_bytes=48 << 20
        ),
        name="network",
    )(
        pair_list,
        pair_count,
        positions,
        normals,
        scales.reshape(square),
        displacement,
        pair_list,
        base_aperture.reshape(square),
        storage.reshape(square),
        injection.reshape(square),
        link_offset.reshape(square),
    )
    return traction, pressure.reshape(-1), residual.reshape(-1)


def solution(mesh):
    return jax.shard_map(
        functools.partial(shards, mesh.shape["grp"], mesh.shape["seg"]),
        mesh=mesh,
        in_specs=(
            P(None, ("grp", "seg")),
            P(None, ("grp", "seg")),
            P(("grp", "seg")),
            P(None, ("grp", "seg")),
            P(None, ("grp", "seg")),
            P(("grp", "seg")),
            P(("grp", "seg")),
            P(("grp", "seg")),
            P(("grp", "seg")),
            P(("grp", "seg")),
        ),
        out_specs=(P(None, ("grp", "seg")), P(("grp", "seg")), P(("grp", "seg"))),
        check_vma=False,
    )
```

```python
import functools

import jax
import jax.numpy as jnp
from jax import lax
from jax.experimental import pallas as pl
from jax.experimental.pallas import tpu as pltpu
from jax.sharding import PartitionSpec as P

BLK = 128
NB = 32
PMAX = 160
F32 = jnp.float32
BF16 = jnp.bfloat16
MESH = pl.DeviceIdType.MESH
NT = (((1,), (1,)), ((), ()))
UNROLL = 16


def split(x, parts):
    out = []
    for _ in range(parts - 1):
        top = x.astype(BF16).astype(F32)
        out.append(top)
        x = x - top
    return out + [x]


def quads(vec, last):
    return jnp.concatenate([vec, last, vec, last], 0)


def kernel(
    sizes,
    pos_in,
    nrm_in,
    scl_in,
    dsp_in,
    pair_in,
    count_in,
    base_in,
    sto_in,
    inj_in,
    off_in,
    traction,
    pressure,
    residual,
    pos,
    nrm,
    scl,
    dsp,
    pairs,
    pair_rows,
    count,
    base,
    sto,
    off,
    prev_pos,
    prev_nrm,
    prev_scl,
    prev_dsp,
    base_next,
    table_inj,
    tfeat,
    sfeat,
    dfeat,
    columns,
    held,
    con_t,
    con_s,
    near0,
    near12,
    got0,
    got0_far,
    got12,
    onehot,
    lanes_hot,
    rows_hot,
    spread,
    table,
    landed_out,
    landed_in,
    part_out,
    part_in,
    landed2_out,
    landed2_in,
    sums_out,
    sums_near,
    sums_far,
    send_sem,
    recv_sem,
    red_send,
    red_recv,
    load_sem,
):
    x_size, core_size, high_size, low_size = sizes
    grp_size, seg_size = x_size * core_size, high_size * low_size
    devices = grp_size * seg_size
    grp = lax.axis_index("grp")
    seg = lax.axis_index("seg")
    me = grp * seg_size + seg

    def device(shift):
        to = lax.rem(me + shift + devices, devices)
        return (to // seg_size, lax.rem(to, seg_size))

    def ring(index, size, low, shift):
        digit = index // low
        if size * low > 1:
            digit = lax.rem(digit, size)
        return index + (lax.rem(digit + shift, size) - digit) * low

    def mate(stage, j):
        if stage == 0:
            return (ring(grp, core_size, 1, j % core_size), ring(seg, low_size, 1, j // core_size))
        return (
            ring(grp, x_size, core_size, j % x_size),
            ring(seg, high_size, low_size, j // x_size),
        )

    groups = (core_size * low_size, x_size * high_size)
    mates = [device(shift) for shift in (1, -1, 2, -2)]
    mates += [mate(stage, j) for stage in (0, 1) for j in range(1, groups[stage])]
    barrier = pltpu.get_barrier_semaphore()
    for to in mates:
        pl.semaphore_signal(barrier, inc=1, device_id=to, device_id_type=MESH)
    loads = {}
    for slot, (src, dst) in enumerate(
        (
            (pos_in, pos),
            (nrm_in, nrm),
            (scl_in, scl),
            (dsp_in, dsp),
            (pair_in, pairs),
            (pair_in, pair_rows),
            (count_in, count),
            (inj_in, table_inj.at[pl.ds(0, NB)]),
            (off_in, off),
            (base_in, base),
            (sto_in, sto),
        )
    ):
        loads[slot] = pltpu.make_async_copy(src, dst, load_sem.at[slot])
        loads[slot].start()
    pl.semaphore_wait(barrier, len(mates))

    def send(src, dst, slot, to):
        copy = pltpu.make_async_remote_copy(
            src_ref=src,
            dst_ref=dst,
            send_sem=send_sem.at[slot],
            recv_sem=recv_sem.at[slot],
            device_id=to,
            device_id_type=MESH,
        )
        copy.start()
        return copy

    after, before, before2 = device(1), device(-1), device(-2)
    frame = [
        send(pos_in, prev_pos, 0, after),
        send(nrm_in, prev_nrm, 1, after),
        send(scl_in, prev_scl, 2, after),
        send(dsp_in, prev_dsp, 3, after),
    ]
    early = [
        send(base_in, base_next, 4, before),
        send(inj_in, table_inj.at[pl.ds(NB, NB)], 5, before),
    ]

    for load in loads.values():
        load.wait()

    row = lax.broadcasted_iota(jnp.int32, (8, BLK), 0)
    low4 = row < 4
    is3 = row == 3
    is7 = row == 7
    is_norm = is3 | is7
    zeros8 = jnp.zeros((8, BLK), F32)
    centre = jnp.mean(pos[...], axis=1, keepdims=True)

    def target_block(k, _):
        lane = pl.ds(pl.multiple_of(k * BLK, BLK), BLK)
        p = pos[:, lane] - centre
        q = quads(p, jnp.sum(p * p, axis=0, keepdims=True))
        q1, q2, q3 = split(jnp.where(is_norm, q, -2.0 * q), 3)
        s = scl[pl.ds(k, 1), :]
        r = quads(nrm[:, lane] * s * 0.125, 0.25 * s)
        r1, r2, r3 = split(r, 3)
        rows = [
            jnp.where(is7, 1.0, q1),
            jnp.where(is7, 1.0, q2),
            jnp.where(is7, 1.0, jnp.where(low4, q3, q1)),
            r1,
            r2,
            jnp.where(low4, r3, r1),
        ]
        d = dsp[:, lane]
        rows += [jnp.concatenate([d, jnp.zeros((5, BLK), F32)], 0)]
        rows += [zeros8] * 9
        upright = jnp.concatenate(rows, 0).T
        tfeat[k] = upright[:, :48].astype(BF16)
        for c in range(3):
            columns[k, c] = jnp.broadcast_to(upright[:, 48 + c : 49 + c], (BLK, BLK))
        return 0

    def source_block(pos_ref, nrm_ref, scl_ref, dsp_ref, first, factor, k, _):
        lane = pl.ds(pl.multiple_of(k * BLK, BLK), BLK)
        p = pos_ref[:, lane] - centre
        q1, q2, q3 = split(quads(p, jnp.sum(p * p, axis=0, keepdims=True) + 0.25), 3)
        s = scl_ref[pl.ds(k, 1), :]
        if factor is not None:
            s = jnp.where(factor, s, 0.0)
        r1, r2, r3 = split(quads(nrm_ref[:, lane] * s, s), 3)
        ahead = [
            jnp.where(is3, 1.0, jnp.where(is7 | low4, q1, q2)),
            jnp.where(is3, 1.0, jnp.where(low4, q1, q2)),
            jnp.where(is3, 1.0, jnp.where(low4, q1, q3)),
            zeros8,
            zeros8,
            zeros8,
        ]
        align = [
            zeros8,
            zeros8,
            zeros8,
            jnp.where(low4, r1, r2),
            jnp.where(low4, r1, r2),
            jnp.where(low4, r1, r3),
        ]
        sfeat[first + k, :, :BLK] = jnp.concatenate(ahead, 0).astype(BF16)
        sfeat[first + k, :, BLK:] = jnp.concatenate(align, 0).astype(BF16)
        d = dsp_ref[:, lane]
        d1, d2 = split(quads(d, jnp.zeros((1, BLK), F32)), 2)
        both = jnp.concatenate([jnp.where(low4, d1, d2), zeros8], 0).astype(BF16)
        dfeat[first + k, :, :BLK] = both
        dfeat[first + k, :, BLK:] = both
        return 0

    lax.fori_loop(0, NB, target_block, 0)
    lax.fori_loop(0, NB, functools.partial(source_block, pos, nrm, scl, dsp, NB, None), 0)

    slot = lax.broadcasted_iota(jnp.int32, (2 * NB, PMAX), 1)
    block = lax.broadcasted_iota(jnp.int32, (2 * NB, PMAX), 0)
    tgt = pair_rows[0:1, :] + NB
    src = pair_rows[1:2, :]
    live = slot < count[0]
    onehot[0] = jnp.where(live & (block == tgt), 1.0, 0.0).astype(BF16)
    onehot[1] = jnp.where(live & (block == src) & (src != tgt), 1.0, 0.0).astype(BF16)

    element = (
        lax.broadcasted_iota(jnp.int32, (NB, BLK), 0) * BLK
        + lax.broadcasted_iota(jnp.int32, (NB, BLK), 1)
    )
    partner = element + off[...]
    part_row = partner >> 7
    part_lane = partner & 127
    inside = jnp.where((me < devices - 1) | (partner < NB * BLK), 0.5, 0.0).astype(F32)
    iota_lane = lax.broadcasted_iota(jnp.int32, (BLK, BLK), 1).astype(F32)
    iota_row = lax.broadcasted_iota(jnp.int32, (2 * NB, BLK), 0)
    upright_lane = part_lane.astype(F32).T
    for k in range(NB):
        lane = pl.ds(k * BLK, BLK)
        lanes_hot[lane, :] = jnp.where(iota_lane == upright_lane[:, k : k + 1], 1.0, 0.0).astype(BF16)
        rows_hot[:, lane] = jnp.where(iota_row == part_row[k : k + 1], 1.0, 0.0).astype(BF16)

    def gather(ref):
        out = []
        for v in range(NB // 8):
            lane = part_lane[8 * v : 8 * v + 8]
            hot = part_row[8 * v : 8 * v + 8]
            acc = jnp.zeros((8, BLK), F32)
            for h in range(8 * v, 8 * v + 8 + NB):
                line = jnp.broadcast_to(ref[h : h + 1, :], (8, BLK))
                got = jnp.take_along_axis(line, lane, axis=1, mode="promise_in_bounds")
                acc = jnp.where(hot == h, got, acc)
            out.append(acc)
        return jnp.concatenate(out, 0)

    def scatter(flux):
        top, rest = split(flux, 2)
        for k in range(NB):
            lane = pl.ds(k * BLK, BLK)
            hot = rows_hot[:, lane]
            for first, x in ((0, top), (2 * NB, rest)):
                line = jnp.broadcast_to(x[k : k + 1], (16, BLK)).astype(BF16)
                spread[first : first + 2 * NB, lane] = hot * jnp.concatenate([line] * 4, 0)
        both = jnp.dot(spread[...], lanes_hot[...], preferred_element_type=F32)
        return both[: 2 * NB] + both[2 * NB :]

    vec = table_inj[:NB, :]
    for copy in early:
        copy.wait_recv()
    vec_diff = vec - gather(table_inj)

    def apply(i, u):
        s = pairs[1, i * UNROLL + u]
        out = lax.dot_general(dfeat[s], held[u], NT, preferred_element_type=F32)
        out = out[:4] + out[4:8]
        for c in range(3):
            con_t[c, i * (UNROLL // 8) + u // 8, u % 8 : u % 8 + 1, :] = out[c : c + 1]

    def evaluate(i, u):
        p = i * UNROLL + u
        t = pairs[0, p]
        m = jnp.dot(tfeat[t], sfeat[pairs[1, p]], preferred_element_type=F32)
        g = m[:, BLK:] * lax.rsqrt(m[:, :BLK])
        top = g.astype(BF16)
        held[u, :, :BLK] = top
        held[u, :, BLK:] = (g - top.astype(F32)).astype(BF16)
        for c in range(3):
            con_s[c, i * (UNROLL // 8) + u // 8, u % 8 : u % 8 + 1, :] = jnp.sum(
                g * columns[t, c], axis=0, keepdims=True
            )

    def steps(i, _):
        for u in range(UNROLL):
            apply(i - 1, u)
            evaluate(i, u)
        return 0

    for u in range(UNROLL):
        evaluate(0, u)
    lax.fori_loop(1, NB // UNROLL, steps, 0)
    for copy in frame:
        copy.wait_recv()
    lax.fori_loop(
        0, NB, functools.partial(source_block, prev_pos, prev_nrm, prev_scl, prev_dsp, 0, me > 0), 0
    )
    lax.fori_loop(NB // UNROLL, PMAX // UNROLL, steps, 0)
    for u in range(UNROLL):
        apply(PMAX // UNROLL - 1, u)

    def blocks(parts):
        out = jnp.zeros((2 * NB, BLK * len(parts)), F32)
        for which, ref in ((0, con_t), (1, con_s)):
            x = jnp.concatenate([ref[c].reshape(PMAX, BLK) for c in parts], 1)
            for y in split(x, 2):
                out = out + jnp.dot(onehot[which], y.astype(BF16), preferred_element_type=F32)
        return out

    first = blocks((0,))
    near0[...] = first
    move0 = [send(near0, got0, 6, before), send(near0.at[pl.ds(0, NB)], got0_far, 7, before2)]
    others = blocks((1, 2))
    near12[0] = others[:NB, :BLK]
    near12[1] = others[:NB, BLK:]
    move12 = send(near12, got12, 8, before)

    def cubed(scale, t):
        aperture = scale * (1.0 + 0.5 * jnp.tanh(t))
        return aperture * aperture * aperture

    for copy in move0:
        copy.wait_recv()
    traction0 = first[NB:] + got0[:NB, :]
    cube = cubed(base[...], traction0)
    table[:NB, :] = cube
    table[NB:, :] = cubed(base_next[...], got0[NB:, :] + got0_far[...])
    weight = inside * (cube + gather(table))

    flux = weight * vec_diff
    landed = scatter(flux)
    part = sto[...] * vec + flux - landed[:NB]
    landed_out[...] = landed[NB:]
    part_out[...] = part
    move_q = [send(landed_out, landed_in, 9, after), send(part_out, part_in, 10, before)]
    for copy in move_q:
        copy.wait_recv()
    q = part - landed_in[...]
    table[:NB, :] = q
    table[NB:, :] = part_in[...] - landed[NB:]
    q_diff = q - gather(table)
    flux = weight * q_diff

    def line(x):
        return jnp.sum(x, axis=0, keepdims=True)

    rows = [line(vec * vec), line(vec * q), line(q * q), line(sto[...] * q * q + flux * q_diff)]
    sums = jnp.concatenate(rows + [jnp.zeros((4, BLK), F32)], 0)

    def distance(stage, j):
        if stage == 0:
            wide, narrow, far = low_size, core_size, j // core_size
        else:
            wide, narrow, far = high_size, x_size, j // x_size
        near = j % narrow
        return min(far, wide - far) + min(near, narrow - near)

    def exchange(stage, sums, got):
        sums_out[stage] = sums
        order = sorted(range(1, groups[stage]), key=functools.partial(distance, stage))
        for j in order[::-1]:
            pltpu.make_async_remote_copy(
                src_ref=sums_out.at[stage],
                dst_ref=got.at[j - 1],
                send_sem=red_send.at[stage],
                recv_sem=red_recv.at[stage],
                device_id=mate(stage, j),
                device_id_type=MESH,
            ).start()

    def collect(stage, sums, got):
        pltpu.make_async_copy(got, got, red_recv.at[stage]).wait()
        parts = [sums] + [got[j] for j in range(groups[stage] - 1)]
        while len(parts) > 1:
            parts = [sum(parts[j : j + 2]) for j in range(0, len(parts), 2)]
        return parts[0]

    exchange(0, sums, sums_near)
    landed = scatter(flux)
    landed2_out[...] = landed[NB:]
    move_u = send(landed2_out, landed2_in, 11, after)
    u_part = sto[...] * q + flux - landed[:NB]
    sums = collect(0, sums, sums_near)
    exchange(1, sums, sums_far)
    move12.wait_recv()
    full = [
        traction0,
        others[NB:, :BLK] + got12[0],
        others[NB:, BLK:] + got12[1],
    ]
    for k in range(NB):
        rows = [x[k : k + 1] for x in full]
        traction[:, pl.ds(k * BLK, BLK)] = jnp.concatenate(rows, 0)
    move_u.wait_recv()
    u = u_part - landed2_in[...]
    sums = collect(1, sums, sums_far)

    total = jnp.sum(sums, axis=1, keepdims=True)
    rr0, r0q, qq, qu = (total[j : j + 1] for j in range(4))
    alpha0 = rr0 / r0q
    rr1 = alpha0 * alpha0 * qq - rr0
    beta = rr1 / rr0
    alpha1 = rr1 / (r0q - 2.0 * alpha0 * qq + alpha0 * alpha0 * qu - beta * rr1 / alpha0)
    keep = 1.0 + beta
    r1 = vec - alpha0 * q
    residual[...] = r1 - alpha1 * (keep * q - alpha0 * u)
    pressure[...] = alpha0 * vec + alpha1 * (r1 + beta * vec)

    for copy in frame + early + move0 + [move12] + move_q + [move_u]:
        copy.wait_send()
    pltpu.make_async_copy(sums_near, sums_near, red_send.at[0]).wait()
    pltpu.make_async_copy(sums_far, sums_far, red_send.at[1]).wait()


def deliver(traction_in, pressure_in, residual_in, traction, pressure, residual, sem):
    refs = ((traction_in, traction), (pressure_in, pressure), (residual_in, residual))
    copies = [pltpu.make_async_copy(a, b, sem.at[j]) for j, (a, b) in enumerate(refs)]
    for copy in copies:
        copy.start()
    for copy in copies:
        copy.wait()


def shards(
    grp_size,
    seg_size,
    positions,
    normals,
    scales,
    displacement,
    pair_list,
    pair_count,
    base_aperture,
    storage,
    injection,
    link_offset,
):
    low_size = 8 if seg_size % 8 == 0 else 2
    high_size = seg_size // low_size
    sizes = (grp_size // 2, 2, high_size, low_size)
    square = (NB, BLK)
    vmem = pl.BlockSpec(memory_space=pltpu.VMEM)
    anywhere = pl.BlockSpec(memory_space=pl.ANY)
    scratch = [
        pltpu.VMEM((3, NB * BLK), F32),
        pltpu.VMEM((3, NB * BLK), F32),
        pltpu.VMEM(square, F32),
        pltpu.VMEM((3, NB * BLK), F32),
        pltpu.SMEM((2, PMAX), jnp.int32),
        pltpu.VMEM((2, PMAX), jnp.int32),
        pltpu.SMEM((1,), jnp.int32),
        pltpu.VMEM(square, F32),
        pltpu.VMEM(square, F32),
        pltpu.VMEM(square, jnp.int32),
        pltpu.VMEM((3, NB * BLK), F32),
        pltpu.VMEM((3, NB * BLK), F32),
        pltpu.VMEM(square, F32),
        pltpu.VMEM((3, NB * BLK), F32),
        pltpu.VMEM(square, F32),
        pltpu.VMEM((2 * NB, BLK), F32),
        pltpu.VMEM((NB, BLK, 48), BF16),
        pltpu.VMEM((2 * NB, 48, 2 * BLK), BF16),
        pltpu.VMEM((2 * NB, 16, 2 * BLK), BF16),
        pltpu.VMEM((NB, 3, BLK, BLK), F32),
        pltpu.VMEM((UNROLL, BLK, 2 * BLK), BF16),
        pltpu.VMEM((3, PMAX // 8, 8, BLK), F32),
        pltpu.VMEM((3, PMAX // 8, 8, BLK), F32),
        pltpu.VMEM((2 * NB, BLK), F32),
        pltpu.VMEM((2, NB, BLK), F32),
        pltpu.VMEM((2 * NB, BLK), F32),
        pltpu.VMEM(square, F32),
        pltpu.VMEM((2, NB, BLK), F32),
        pltpu.VMEM((2, 2 * NB, PMAX), BF16),
        pltpu.VMEM((NB * BLK, BLK), BF16),
        pltpu.VMEM((2 * NB, NB * BLK), BF16),
        pltpu.VMEM((4 * NB, NB * BLK), BF16),
        pltpu.VMEM((2 * NB, BLK), F32),
        pltpu.VMEM(square, F32),
        pltpu.VMEM(square, F32),
        pltpu.VMEM(square, F32),
        pltpu.VMEM(square, F32),
        pltpu.VMEM(square, F32),
        pltpu.VMEM(square, F32),
        pltpu.VMEM((2, 8, BLK), F32),
        pltpu.VMEM((2 * low_size - 1, 8, BLK), F32),
        pltpu.VMEM((grp_size // 2 * high_size - 1, 8, BLK), F32),
        pltpu.SemaphoreType.DMA((12,)),
        pltpu.SemaphoreType.DMA((12,)),
        pltpu.SemaphoreType.DMA((2,)),
        pltpu.SemaphoreType.DMA((2,)),
        pltpu.SemaphoreType.DMA((11,)),
    ]
    shapes = (
        jax.ShapeDtypeStruct((3, NB * BLK), F32),
        jax.ShapeDtypeStruct(square, F32),
        jax.ShapeDtypeStruct(square, F32),
    )
    outs = pl.pallas_call(
        functools.partial(kernel, sizes),
        out_shape=shapes,
        in_specs=[anywhere] * 10,
        out_specs=(vmem, vmem, vmem),
        scratch_shapes=scratch,
        compiler_params=pltpu.CompilerParams(
            collective_id=0, has_side_effects=True, vmem_limit_bytes=56 << 20
        ),
        name="network",
    )(
        positions,
        normals,
        scales.reshape(square),
        displacement,
        pair_list,
        pair_count,
        base_aperture.reshape(square),
        storage.reshape(square),
        injection.reshape(square),
        link_offset.reshape(square),
    )
    traction, pressure, residual = pl.pallas_call(
        deliver,
        out_shape=shapes,
        in_specs=[vmem] * 3,
        out_specs=(anywhere,) * 3,
        scratch_shapes=[pltpu.SemaphoreType.DMA((3,))],
        name="deliver",
    )(*outs)
    return traction, pressure.reshape(-1), residual.reshape(-1)


def solution(mesh):
    return jax.shard_map(
        functools.partial(shards, mesh.shape["grp"], mesh.shape["seg"]),
        mesh=mesh,
        in_specs=(
            P(None, ("grp", "seg")),
            P(None, ("grp", "seg")),
            P(("grp", "seg")),
            P(None, ("grp", "seg")),
            P(None, ("grp", "seg")),
            P(("grp", "seg")),
            P(("grp", "seg")),
            P(("grp", "seg")),
            P(("grp", "seg")),
            P(("grp", "seg")),
        ),
        out_specs=(P(None, ("grp", "seg")), P(("grp", "seg")), P(("grp", "seg"))),
        check_vma=False,
    )
```

```python
import functools

import jax
import jax.numpy as jnp
from jax import lax
from jax.experimental import pallas as pl
from jax.experimental.pallas import tpu as pltpu
from jax.sharding import PartitionSpec as P

BLK = 128
NB = 32
PMAX = 160
F32 = jnp.float32
BF16 = jnp.bfloat16
MESH = pl.DeviceIdType.MESH
NT = (((1,), (1,)), ((), ()))
UNROLL = 16


def split(x, parts):
    out = []
    for _ in range(parts - 1):
        top = x.astype(BF16).astype(F32)
        out.append(top)
        x = x - top
    return out + [x]


def quads(vec, last):
    return jnp.concatenate([vec, last, vec, last], 0)


def kernel(
    sizes,
    pos_in,
    nrm_in,
    scl_in,
    dsp_in,
    pair_in,
    count_in,
    base_in,
    sto_in,
    inj_in,
    off_in,
    traction,
    pressure,
    residual,
    pos,
    nrm,
    scl,
    dsp,
    pairs,
    pair_rows,
    count,
    bases,
    stores,
    offs,
    prev_pos,
    prev_nrm,
    prev_scl,
    prev_dsp,
    table_inj,
    tfeat,
    sfeat,
    dfeat,
    columns,
    held,
    con_t,
    con_s,
    near0,
    near12,
    got_prev,
    got_next,
    got_next2,
    got_next3,
    got12,
    onehot,
    lanes_hot,
    rows_hot,
    spread,
    table,
    landed_out,
    landed_in,
    sums_out,
    sums_near,
    sums_far,
    send_sem,
    recv_sem,
    red_send,
    red_recv,
    load_sem,
):
    x_size, core_size, high_size, low_size = sizes
    grp_size, seg_size = x_size * core_size, high_size * low_size
    devices = grp_size * seg_size
    grp = lax.axis_index("grp")
    seg = lax.axis_index("seg")
    me = grp * seg_size + seg

    def device(shift):
        to = lax.rem(me + shift + devices, devices)
        return (to // seg_size, lax.rem(to, seg_size))

    def ring(index, size, low, shift):
        digit = index // low
        if size * low > 1:
            digit = lax.rem(digit, size)
        return index + (lax.rem(digit + shift, size) - digit) * low

    def mate(stage, j):
        if stage == 0:
            return (ring(grp, core_size, 1, j % core_size), ring(seg, low_size, 1, j // core_size))
        return (
            ring(grp, x_size, core_size, j % x_size),
            ring(seg, high_size, low_size, j // x_size),
        )

    groups = (core_size * low_size, x_size * high_size)
    mates = [device(shift) for shift in (1, -1, 2, -2, 3, -3)]
    mates += [mate(stage, j) for stage in (0, 1) for j in range(1, groups[stage])]
    barrier = pltpu.get_barrier_semaphore()
    for to in mates:
        pl.semaphore_signal(barrier, inc=1, device_id=to, device_id_type=MESH)
    loads = {}
    for slot, (src, dst) in enumerate(
        (
            (pos_in, pos),
            (nrm_in, nrm),
            (scl_in, scl),
            (dsp_in, dsp),
            (pair_in, pairs),
            (pair_in, pair_rows),
            (count_in, count),
            (inj_in, table_inj.at[pl.ds(NB, NB)]),
            (off_in, offs.at[1]),
            (base_in, bases.at[1]),
            (sto_in, stores.at[0]),
        )
    ):
        loads[slot] = pltpu.make_async_copy(src, dst, load_sem.at[slot])
        loads[slot].start()
    pl.semaphore_wait(barrier, len(mates))

    def send(src, dst, slot, to):
        copy = pltpu.make_async_remote_copy(
            src_ref=src,
            dst_ref=dst,
            send_sem=send_sem.at[slot],
            recv_sem=recv_sem.at[slot],
            device_id=to,
            device_id_type=MESH,
        )
        copy.start()
        return copy

    after, before, before2, before3 = (device(shift) for shift in (1, -1, -2, -3))
    frame = [
        send(pos_in, prev_pos, 0, after),
        send(nrm_in, prev_nrm, 1, after),
        send(scl_in, prev_scl, 2, after),
        send(dsp_in, prev_dsp, 3, after),
    ]
    early = [
        send(inj_in, table_inj.at[pl.ds(2 * NB, NB)], 4, before),
        send(off_in, offs.at[2], 5, before),
        send(base_in, bases.at[2], 6, before),
        send(sto_in, stores.at[1], 7, before),
        send(inj_in, table_inj.at[pl.ds(3 * NB, NB)], 8, before2),
        send(base_in, bases.at[3], 9, before2),
    ]
    for load in loads.values():
        load.wait()

    row = lax.broadcasted_iota(jnp.int32, (8, BLK), 0)
    low4 = row < 4
    is3 = row == 3
    is7 = row == 7
    is_norm = is3 | is7
    zeros8 = jnp.zeros((8, BLK), F32)
    centre = jnp.mean(pos[...], axis=1, keepdims=True)

    def target_block(k, _):
        lane = pl.ds(pl.multiple_of(k * BLK, BLK), BLK)
        p = pos[:, lane] - centre
        q = quads(p, jnp.sum(p * p, axis=0, keepdims=True))
        q1, q2, q3 = split(jnp.where(is_norm, q, -2.0 * q), 3)
        s = scl[pl.ds(k, 1), :]
        r = quads(nrm[:, lane] * s * 0.125, 0.25 * s)
        r1, r2, r3 = split(r, 3)
        rows = [
            jnp.where(is7, 1.0, q1),
            jnp.where(is7, 1.0, q2),
            jnp.where(is7, 1.0, jnp.where(low4, q3, q1)),
            r1,
            r2,
            jnp.where(low4, r3, r1),
        ]
        d = dsp[:, lane]
        rows += [jnp.concatenate([d, jnp.zeros((5, BLK), F32)], 0)]
        rows += [zeros8] * 9
        upright = jnp.concatenate(rows, 0).T
        tfeat[k] = upright[:, :48].astype(BF16)
        for c in range(3):
            columns[k, c] = jnp.broadcast_to(upright[:, 48 + c : 49 + c], (BLK, BLK))
        return 0

    def source_block(pos_ref, nrm_ref, scl_ref, dsp_ref, first, factor, k, _):
        lane = pl.ds(pl.multiple_of(k * BLK, BLK), BLK)
        p = pos_ref[:, lane] - centre
        q1, q2, q3 = split(quads(p, jnp.sum(p * p, axis=0, keepdims=True) + 0.25), 3)
        s = scl_ref[pl.ds(k, 1), :]
        if factor is not None:
            s = jnp.where(factor, s, 0.0)
        r1, r2, r3 = split(quads(nrm_ref[:, lane] * s, s), 3)
        ahead = [
            jnp.where(is3, 1.0, jnp.where(is7 | low4, q1, q2)),
            jnp.where(is3, 1.0, jnp.where(low4, q1, q2)),
            jnp.where(is3, 1.0, jnp.where(low4, q1, q3)),
            zeros8,
            zeros8,
            zeros8,
        ]
        align = [
            zeros8,
            zeros8,
            zeros8,
            jnp.where(low4, r1, r2),
            jnp.where(low4, r1, r2),
            jnp.where(low4, r1, r3),
        ]
        sfeat[first + k, :, :BLK] = jnp.concatenate(ahead, 0).astype(BF16)
        sfeat[first + k, :, BLK:] = jnp.concatenate(align, 0).astype(BF16)
        d = dsp_ref[:, lane]
        d1, d2 = split(quads(d, jnp.zeros((1, BLK), F32)), 2)
        both = jnp.concatenate([jnp.where(low4, d1, d2), zeros8], 0).astype(BF16)
        dfeat[first + k, :, :BLK] = both
        dfeat[first + k, :, BLK:] = both
        return 0

    lax.fori_loop(0, NB, target_block, 0)
    lax.fori_loop(0, NB, functools.partial(source_block, pos, nrm, scl, dsp, NB, None), 0)

    slot = lax.broadcasted_iota(jnp.int32, (2 * NB, PMAX), 1)
    block = lax.broadcasted_iota(jnp.int32, (2 * NB, PMAX), 0)
    tgt = pair_rows[0:1, :] + NB
    src = pair_rows[1:2, :]
    live = slot < count[0]
    onehot[0] = jnp.where(live & (block == tgt), 1.0, 0.0).astype(BF16)
    onehot[1] = jnp.where(live & (block == src) & (src != tgt), 1.0, 0.0).astype(BF16)

    def apply(i, u):
        s = pairs[1, i * UNROLL + u]
        out = lax.dot_general(dfeat[s], held[u], NT, preferred_element_type=F32)
        out = out[:4] + out[4:8]
        for c in range(3):
            con_t[c, i * (UNROLL // 8) + u // 8, u % 8 : u % 8 + 1, :] = out[c : c + 1]

    def evaluate(i, u):
        p = i * UNROLL + u
        t = pairs[0, p]
        m = jnp.dot(tfeat[t], sfeat[pairs[1, p]], preferred_element_type=F32)
        g = m[:, BLK:] * lax.rsqrt(m[:, :BLK])
        top = g.astype(BF16)
        held[u, :, :BLK] = top
        held[u, :, BLK:] = (g - top.astype(F32)).astype(BF16)
        for c in range(3):
            con_s[c, i * (UNROLL // 8) + u // 8, u % 8 : u % 8 + 1, :] = jnp.sum(
                g * columns[t, c], axis=0, keepdims=True
            )

    def steps(i, _):
        for u in range(UNROLL):
            apply(i - 1, u)
            evaluate(i, u)
        return 0

    for u in range(UNROLL):
        evaluate(0, u)
    lax.fori_loop(1, NB // UNROLL, steps, 0)
    for copy in frame:
        copy.wait_recv()
    early += [
        send(inj_in, table_inj.at[pl.ds(0, NB)], 10, after),
        send(off_in, offs.at[0], 11, after),
        send(base_in, bases.at[0], 12, after),
    ]
    lax.fori_loop(
        0, NB, functools.partial(source_block, prev_pos, prev_nrm, prev_scl, prev_dsp, 0, me > 0), 0
    )
    lax.fori_loop(NB // UNROLL, PMAX // UNROLL, steps, 0)
    for u in range(UNROLL):
        apply(PMAX // UNROLL - 1, u)

    def blocks(parts):
        out = jnp.zeros((2 * NB, BLK * len(parts)), F32)
        for which, ref in ((0, con_t), (1, con_s)):
            x = jnp.concatenate([ref[c].reshape(PMAX, BLK) for c in parts], 1)
            for y in split(x, 2):
                out = out + jnp.dot(onehot[which], y.astype(BF16), preferred_element_type=F32)
        return out

    first = blocks((0,))
    near0[...] = first
    move0 = [
        send(near0.at[pl.ds(0, NB)], got_next3, 13, before3),
        send(near0, got_next2, 14, before2),
        send(near0, got_next, 15, before),
        send(near0.at[pl.ds(NB, NB)], got_prev, 16, after),
    ]
    others = blocks((1, 2))
    near12[0] = others[:NB, :BLK]
    near12[1] = others[:NB, BLK:]
    move12 = send(near12, got12, 17, before)

    element = (
        lax.broadcasted_iota(jnp.int32, (NB, BLK), 0) * BLK
        + lax.broadcasted_iota(jnp.int32, (NB, BLK), 1)
    )
    iota_lane = lax.broadcasted_iota(jnp.int32, (BLK, BLK), 1).astype(F32)
    hot_first = (0, NB, 3 * NB)
    hot_rows = ((NB, 2 * NB), (0, 2 * NB), (0, NB))
    part_row, part_lane, inside = [], [], []
    for copy in early:
        copy.wait_recv()
    for e in range(3):
        partner = element + offs[e]
        part_row.append(partner >> 7)
        part_lane.append(partner & 127)
        if e == 0:
            kept = me > 0
        else:
            kept = (me < devices - e) | (partner < NB * BLK)
        inside.append(jnp.where(kept, 0.5, 0.0).astype(F32))
        begin, end = hot_rows[e]
        iota_row = lax.broadcasted_iota(jnp.int32, (end - begin, BLK), 0) + begin
        upright_lane = part_lane[e].astype(F32).T
        for k in range(NB):
            lane = pl.ds(k * BLK, BLK)
            lanes_hot[e, lane, :] = jnp.where(
                iota_lane == upright_lane[:, k : k + 1], 1.0, 0.0
            ).astype(BF16)
            rows_hot[hot_first[e] : hot_first[e] + end - begin, lane] = jnp.where(
                iota_row == part_row[e][k : k + 1], 1.0, 0.0
            ).astype(BF16)

    def gather(ref, e):
        out = []
        for v in range(NB // 8):
            lane = part_lane[e][8 * v : 8 * v + 8]
            hot = part_row[e][8 * v : 8 * v + 8]
            acc = jnp.zeros((8, BLK), F32)
            for h in range(8 * v, 8 * v + 8 + NB):
                line = jnp.broadcast_to(ref[NB * e + h : NB * e + h + 1, :], (8, BLK))
                got = jnp.take_along_axis(line, lane, axis=1, mode="promise_in_bounds")
                acc = jnp.where(hot == h, got, acc)
            out.append(acc)
        return jnp.concatenate(out, 0)

    def scatter(flux, e):
        size = hot_rows[e][1] - hot_rows[e][0]
        hot_at = hot_first[e]
        at = 2 * hot_at
        for k in range(NB):
            lane = pl.ds(k * BLK, BLK)
            hot = rows_hot[hot_at : hot_at + size, lane]
            for first_row, x in zip((at, at + size), split(flux, 2)):
                line = jnp.broadcast_to(x[k : k + 1], (16, BLK)).astype(BF16)
                line = jnp.concatenate([line] * (size // 16), 0)
                spread[first_row : first_row + size, lane] = hot * line
        both = jnp.dot(spread[at : at + 2 * size, :], lanes_hot[e], preferred_element_type=F32)
        return both[:size] + both[size:]

    vecs = [table_inj[NB * e : NB * (e + 1), :] for e in range(3)]
    diffs = [vecs[e] - gather(table_inj, e) for e in range(3)]
    vec, sto = vecs[1], stores[0]

    def cubed(scale, t):
        aperture = scale * (1.0 + 0.5 * jnp.tanh(t))
        return aperture * aperture * aperture

    for copy in move0:
        copy.wait_recv()
    traction0 = first[NB:] + got_next[:NB, :]
    cubes = [
        cubed(bases[0], got_prev[...] + first[:NB]),
        cubed(bases[1], traction0),
        cubed(bases[2], got_next[NB:, :] + got_next2[:NB, :]),
        cubed(bases[3], got_next2[NB:, :] + got_next3[...]),
    ]
    for e in range(4):
        table[NB * e : NB * (e + 1), :] = cubes[e]
    weights = [inside[e] * (cubes[e] + gather(table, e)) for e in range(3)]
    weight = weights[1]
    fluxes = [weights[e] * diffs[e] for e in range(3)]
    landed = [scatter(fluxes[e], e) for e in range(3)]
    q = sto * vec + fluxes[1] - landed[1][:NB] - landed[0]
    q_next = stores[1] * vecs[2] + fluxes[2] - landed[2] - landed[1][NB:]
    table[NB : 2 * NB, :] = q
    table[2 * NB : 3 * NB, :] = q_next
    q_diff = q - gather(table, 1)
    flux = weight * q_diff

    def line(x):
        return jnp.sum(x, axis=0, keepdims=True)

    rows = [line(vec * vec), line(vec * q), line(q * q), line(sto * q * q + flux * q_diff)]
    sums = jnp.concatenate(rows + [jnp.zeros((4, BLK), F32)], 0)

    def distance(stage, j):
        if stage == 0:
            wide, narrow, far = low_size, core_size, j // core_size
        else:
            wide, narrow, far = high_size, x_size, j // x_size
        near = j % narrow
        return min(far, wide - far) + min(near, narrow - near)

    def exchange(stage, sums, got):
        sums_out[stage] = sums
        order = sorted(range(1, groups[stage]), key=functools.partial(distance, stage))
        for j in order[::-1]:
            pltpu.make_async_remote_copy(
                src_ref=sums_out.at[stage],
                dst_ref=got.at[j - 1],
                send_sem=red_send.at[stage],
                recv_sem=red_recv.at[stage],
                device_id=mate(stage, j),
                device_id_type=MESH,
            ).start()

    def collect(stage, sums, got):
        pltpu.make_async_copy(got, got, red_recv.at[stage]).wait()
        parts = [sums] + [got[j] for j in range(groups[stage] - 1)]
        while len(parts) > 1:
            parts = [sum(parts[j : j + 2]) for j in range(0, len(parts), 2)]
        return parts[0]

    exchange(0, sums, sums_near)
    landed = scatter(flux, 1)
    landed_out[...] = landed[NB:]
    move_u = send(landed_out, landed_in, 18, after)
    u_part = sto * q + flux - landed[:NB]
    sums = collect(0, sums, sums_near)
    exchange(1, sums, sums_far)
    move12.wait_recv()
    full = [
        traction0,
        others[NB:, :BLK] + got12[0],
        others[NB:, BLK:] + got12[1],
    ]
    for k in range(NB):
        rows = [x[k : k + 1] for x in full]
        traction[:, pl.ds(k * BLK, BLK)] = jnp.concatenate(rows, 0)
    move_u.wait_recv()
    u = u_part - landed_in[...]
    sums = collect(1, sums, sums_far)

    total = jnp.sum(sums, axis=1, keepdims=True)
    rr0, r0q, qq, qu = (total[j : j + 1] for j in range(4))
    alpha0 = rr0 / r0q
    rr1 = alpha0 * alpha0 * qq - rr0
    beta = rr1 / rr0
    alpha1 = rr1 / (r0q - 2.0 * alpha0 * qq + alpha0 * alpha0 * qu - beta * rr1 / alpha0)
    keep = 1.0 + beta
    r1 = vec - alpha0 * q
    residual[...] = r1 - alpha1 * (keep * q - alpha0 * u)
    pressure[...] = alpha0 * vec + alpha1 * (r1 + beta * vec)

    for copy in frame + early + move0 + [move12, move_u]:
        copy.wait_send()
    pltpu.make_async_copy(sums_near, sums_near, red_send.at[0]).wait()
    pltpu.make_async_copy(sums_far, sums_far, red_send.at[1]).wait()


def deliver(traction_in, pressure_in, residual_in, traction, pressure, residual, sem):
    refs = ((traction_in, traction), (pressure_in, pressure), (residual_in, residual))
    copies = [pltpu.make_async_copy(a, b, sem.at[j]) for j, (a, b) in enumerate(refs)]
    for copy in copies:
        copy.start()
    for copy in copies:
        copy.wait()


def shards(
    grp_size,
    seg_size,
    positions,
    normals,
    scales,
    displacement,
    pair_list,
    pair_count,
    base_aperture,
    storage,
    injection,
    link_offset,
):
    low_size = 8 if seg_size % 8 == 0 else 2
    high_size = seg_size // low_size
    sizes = (grp_size // 2, 2, high_size, low_size)
    square = (NB, BLK)
    vmem = pl.BlockSpec(memory_space=pltpu.VMEM)
    anywhere = pl.BlockSpec(memory_space=pl.ANY)
    rows3 = pltpu.VMEM((3, NB * BLK), F32)
    tile = pltpu.VMEM(square, F32)
    double = pltpu.VMEM((2 * NB, BLK), F32)
    scratch = [
        rows3,
        rows3,
        tile,
        rows3,
        pltpu.SMEM((2, PMAX), jnp.int32),
        pltpu.VMEM((2, PMAX), jnp.int32),
        pltpu.SMEM((1,), jnp.int32),
        pltpu.VMEM((4, NB, BLK), F32),
        pltpu.VMEM((2, NB, BLK), F32),
        pltpu.VMEM((3, NB, BLK), jnp.int32),
        rows3,
        rows3,
        tile,
        rows3,
        pltpu.VMEM((4 * NB, BLK), F32),
        pltpu.VMEM((NB, BLK, 48), BF16),
        pltpu.VMEM((2 * NB, 48, 2 * BLK), BF16),
        pltpu.VMEM((2 * NB, 16, 2 * BLK), BF16),
        pltpu.VMEM((NB, 3, BLK, BLK), F32),
        pltpu.VMEM((UNROLL, BLK, 2 * BLK), BF16),
        pltpu.VMEM((3, PMAX // 8, 8, BLK), F32),
        pltpu.VMEM((3, PMAX // 8, 8, BLK), F32),
        double,
        pltpu.VMEM((2, NB, BLK), F32),
        tile,
        double,
        double,
        tile,
        pltpu.VMEM((2, NB, BLK), F32),
        pltpu.VMEM((2, 2 * NB, PMAX), BF16),
        pltpu.VMEM((3, NB * BLK, BLK), BF16),
        pltpu.VMEM((4 * NB, NB * BLK), BF16),
        pltpu.VMEM((8 * NB, NB * BLK), BF16),
        pltpu.VMEM((4 * NB, BLK), F32),
        tile,
        tile,
        pltpu.VMEM((2, 8, BLK), F32),
        pltpu.VMEM((2 * low_size - 1, 8, BLK), F32),
        pltpu.VMEM((grp_size // 2 * high_size - 1, 8, BLK), F32),
        pltpu.SemaphoreType.DMA((19,)),
        pltpu.SemaphoreType.DMA((19,)),
        pltpu.SemaphoreType.DMA((2,)),
        pltpu.SemaphoreType.DMA((2,)),
        pltpu.SemaphoreType.DMA((11,)),
    ]
    shapes = (
        jax.ShapeDtypeStruct((3, NB * BLK), F32),
        jax.ShapeDtypeStruct(square, F32),
        jax.ShapeDtypeStruct(square, F32),
    )
    outs = pl.pallas_call(
        functools.partial(kernel, sizes),
        out_shape=shapes,
        in_specs=[anywhere] * 10,
        out_specs=(vmem, vmem, vmem),
        scratch_shapes=scratch,
        compiler_params=pltpu.CompilerParams(
            collective_id=0, has_side_effects=True, vmem_limit_bytes=56 << 20
        ),
        name="network",
    )(
        positions,
        normals,
        scales.reshape(square),
        displacement,
        pair_list,
        pair_count,
        base_aperture.reshape(square),
        storage.reshape(square),
        injection.reshape(square),
        link_offset.reshape(square),
    )
    traction, pressure, residual = pl.pallas_call(
        deliver,
        out_shape=shapes,
        in_specs=[vmem] * 3,
        out_specs=(anywhere,) * 3,
        scratch_shapes=[pltpu.SemaphoreType.DMA((3,))],
        name="deliver",
    )(*outs)
    return traction, pressure.reshape(-1), residual.reshape(-1)


def solution(mesh):
    return jax.shard_map(
        functools.partial(shards, mesh.shape["grp"], mesh.shape["seg"]),
        mesh=mesh,
        in_specs=(
            P(None, ("grp", "seg")),
            P(None, ("grp", "seg")),
            P(("grp", "seg")),
            P(None, ("grp", "seg")),
            P(None, ("grp", "seg")),
            P(("grp", "seg")),
            P(("grp", "seg")),
            P(("grp", "seg")),
            P(("grp", "seg")),
            P(("grp", "seg")),
        ),
        out_specs=(P(None, ("grp", "seg")), P(("grp", "seg")), P(("grp", "seg"))),
        check_vma=False,
    )
```

```python
import functools

import jax
import jax.numpy as jnp
from jax import lax
from jax.experimental import pallas as pl
from jax.experimental.pallas import tpu as pltpu
from jax.sharding import PartitionSpec as P

BLK = 128
NB = 32
PMAX = 160
F32 = jnp.float32
BF16 = jnp.bfloat16
MESH = pl.DeviceIdType.MESH
NT = (((1,), (1,)), ((), ()))
UNROLL = 16


def split(x, parts):
    out = []
    for _ in range(parts - 1):
        top = x.astype(BF16).astype(F32)
        out.append(top)
        x = x - top
    return out + [x]


def quads(vec, last):
    return jnp.concatenate([vec, last, vec, last], 0)


def kernel(
    sizes,
    pos_in,
    nrm_in,
    scl_in,
    dsp_in,
    pair_in,
    count_in,
    base_in,
    sto_in,
    inj_in,
    off_in,
    traction,
    pressure,
    residual,
    pos,
    nrm,
    scl,
    dsp,
    pairs,
    pair_rows,
    count,
    bases,
    stores,
    offs,
    prev_pos,
    prev_nrm,
    prev_scl,
    prev_dsp,
    table_inj,
    tfeat,
    sfeat,
    dfeat,
    columns,
    held,
    con_t,
    con_s,
    near0,
    near12,
    got_prev,
    got_next,
    got_next2,
    got_next3,
    got12,
    onehot,
    lanes_hot,
    rows_hot,
    spread,
    table,
    landed_out,
    landed_in,
    sums_out,
    sums_near,
    sums_far,
    send_sem,
    recv_sem,
    red_send,
    red_recv,
    load_sem,
):
    x_size, core_size, high_size, low_size = sizes
    grp_size, seg_size = x_size * core_size, high_size * low_size
    devices = grp_size * seg_size
    grp = lax.axis_index("grp")
    seg = lax.axis_index("seg")
    me = grp * seg_size + seg

    def device(shift):
        to = lax.rem(me + shift + devices, devices)
        return (to // seg_size, lax.rem(to, seg_size))

    def ring(index, size, low, shift):
        digit = index // low
        if size * low > 1:
            digit = lax.rem(digit, size)
        return index + (lax.rem(digit + shift, size) - digit) * low

    def mate(stage, j):
        if stage == 0:
            return (ring(grp, core_size, 1, j % core_size), ring(seg, low_size, 1, j // core_size))
        return (
            ring(grp, x_size, core_size, j % x_size),
            ring(seg, high_size, low_size, j // x_size),
        )

    groups = (core_size * low_size, x_size * high_size)
    mates = [device(shift) for shift in (1, -1, 2, -2, 3, -3)]
    mates += [mate(stage, j) for stage in (0, 1) for j in range(1, groups[stage])]
    barrier = pltpu.get_barrier_semaphore()
    for to in mates:
        pl.semaphore_signal(barrier, inc=1, device_id=to, device_id_type=MESH)
    loads = {}
    for slot, (src, dst) in enumerate(
        (
            (pos_in, pos),
            (nrm_in, nrm),
            (scl_in, scl),
            (dsp_in, dsp),
            (pair_in, pairs),
            (pair_in, pair_rows),
            (count_in, count),
            (inj_in, table_inj.at[pl.ds(NB, NB)]),
            (off_in, offs.at[1]),
            (base_in, bases.at[1]),
            (sto_in, stores.at[0]),
        )
    ):
        loads[slot] = pltpu.make_async_copy(src, dst, load_sem.at[slot])
        loads[slot].start()
    pl.semaphore_wait(barrier, len(mates))

    def send(src, dst, slot, to):
        copy = pltpu.make_async_remote_copy(
            src_ref=src,
            dst_ref=dst,
            send_sem=send_sem.at[slot],
            recv_sem=recv_sem.at[slot],
            device_id=to,
            device_id_type=MESH,
        )
        copy.start()
        return copy

    after, before, before2, before3 = (device(shift) for shift in (1, -1, -2, -3))
    frame = [
        send(pos_in, prev_pos, 0, after),
        send(nrm_in, prev_nrm, 1, after),
        send(scl_in, prev_scl, 2, after),
        send(dsp_in, prev_dsp, 3, after),
    ]
    early = [
        send(inj_in, table_inj.at[pl.ds(2 * NB, NB)], 4, before),
        send(off_in, offs.at[2], 5, before),
        send(base_in, bases.at[2], 6, before),
        send(sto_in, stores.at[1], 7, before),
        send(inj_in, table_inj.at[pl.ds(3 * NB, NB)], 8, before2),
        send(base_in, bases.at[3], 9, before2),
    ]
    for slot in range(4):
        loads[slot].wait()

    row = lax.broadcasted_iota(jnp.int32, (8, BLK), 0)
    low4 = row < 4
    is3 = row == 3
    is7 = row == 7
    is_norm = is3 | is7
    zeros8 = jnp.zeros((8, BLK), F32)
    centre = jnp.mean(pos[...], axis=1, keepdims=True)

    def target_block(k):
        lane = pl.ds(pl.multiple_of(k * BLK, BLK), BLK)
        p = pos[:, lane] - centre
        q = quads(p, jnp.sum(p * p, axis=0, keepdims=True))
        q1, q2, q3 = split(jnp.where(is_norm, q, -2.0 * q), 3)
        s = scl[pl.ds(k, 1), :]
        r = quads(nrm[:, lane] * s * 0.125, 0.25 * s)
        r1, r2, r3 = split(r, 3)
        rows = [
            jnp.where(is7, 1.0, q1),
            jnp.where(is7, 1.0, q2),
            jnp.where(is7, 1.0, jnp.where(low4, q3, q1)),
            r1,
            r2,
            jnp.where(low4, r3, r1),
        ]
        d = dsp[:, lane]
        rows += [jnp.concatenate([d, jnp.zeros((5, BLK), F32)], 0)]
        upright = jnp.concatenate(rows, 0).T
        tfeat[k] = upright[:, :48].astype(BF16)
        for c in range(3):
            columns[k, c] = jnp.broadcast_to(upright[:, 48 + c : 49 + c], (BLK, BLK))

    def source_block(pos_ref, nrm_ref, scl_ref, dsp_ref, first, factor, k):
        lane = pl.ds(pl.multiple_of(k * BLK, BLK), BLK)
        p = pos_ref[:, lane] - centre
        q1, q2, q3 = split(quads(p, jnp.sum(p * p, axis=0, keepdims=True) + 0.25), 3)
        s = scl_ref[pl.ds(k, 1), :]
        if factor is not None:
            s = jnp.where(factor, s, 0.0)
        r1, r2, r3 = split(quads(nrm_ref[:, lane] * s, s), 3)
        ahead = [
            jnp.where(is3, 1.0, jnp.where(is7 | low4, q1, q2)),
            jnp.where(is3, 1.0, jnp.where(low4, q1, q2)),
            jnp.where(is3, 1.0, jnp.where(low4, q1, q3)),
            zeros8,
            zeros8,
            zeros8,
        ]
        align = [
            zeros8,
            zeros8,
            zeros8,
            jnp.where(low4, r1, r2),
            jnp.where(low4, r1, r2),
            jnp.where(low4, r1, r3),
        ]
        sfeat[first + k, :, :BLK] = jnp.concatenate(ahead, 0).astype(BF16)
        sfeat[first + k, :, BLK:] = jnp.concatenate(align, 0).astype(BF16)
        d = dsp_ref[:, lane]
        d1, d2 = split(quads(d, jnp.zeros((1, BLK), F32)), 2)
        both = jnp.concatenate([jnp.where(low4, d1, d2), zeros8], 0).astype(BF16)
        dfeat[first + k, :, :BLK] = both
        dfeat[first + k, :, BLK:] = both

    def own_blocks(i, _):
        for j in range(4):
            target_block(4 * i + j)
            source_block(pos, nrm, scl, dsp, NB, None, 4 * i + j)
        return 0

    def prev_blocks(i, _):
        for j in range(8):
            source_block(prev_pos, prev_nrm, prev_scl, prev_dsp, 0, me > 0, 8 * i + j)
        return 0

    lax.fori_loop(0, NB // 4, own_blocks, 0)

    for slot in range(4, 11):
        loads[slot].wait()

    slot = lax.broadcasted_iota(jnp.int32, (2 * NB, PMAX), 1)
    block = lax.broadcasted_iota(jnp.int32, (2 * NB, PMAX), 0)
    tgt = pair_rows[0:1, :] + NB
    src = pair_rows[1:2, :]
    live = slot < count[0]
    onehot[0] = jnp.where(live & (block == tgt), 1.0, 0.0).astype(BF16)
    onehot[1] = jnp.where(live & (block == src) & (src != tgt), 1.0, 0.0).astype(BF16)

    def apply(i, u):
        s = pairs[1, i * UNROLL + u]
        out = lax.dot_general(dfeat[s], held[u], NT, preferred_element_type=F32)
        out = out[:4] + out[4:8]
        for c in range(3):
            con_t[c, i * (UNROLL // 8) + u // 8, u % 8 : u % 8 + 1, :] = out[c : c + 1]

    def evaluate(i, u):
        p = i * UNROLL + u
        t = pairs[0, p]
        m = jnp.dot(tfeat[t], sfeat[pairs[1, p]], preferred_element_type=F32)
        g = m[:, BLK:] * lax.rsqrt(m[:, :BLK])
        top = g.astype(BF16)
        held[u, :, :BLK] = top
        held[u, :, BLK:] = (g - top.astype(F32)).astype(BF16)
        for c in range(3):
            con_s[c, i * (UNROLL // 8) + u // 8, u % 8 : u % 8 + 1, :] = jnp.sum(
                g * columns[t, c], axis=0, keepdims=True
            )

    def steps(i, _):
        for u in range(UNROLL):
            apply(i - 1, u)
            evaluate(i, u)
        return 0

    for u in range(UNROLL):
        evaluate(0, u)
    lax.fori_loop(1, NB // UNROLL, steps, 0)
    for copy in frame:
        copy.wait_recv()
    early += [
        send(inj_in, table_inj.at[pl.ds(0, NB)], 10, after),
        send(off_in, offs.at[0], 11, after),
        send(base_in, bases.at[0], 12, after),
    ]
    lax.fori_loop(0, NB // 8, prev_blocks, 0)
    lax.fori_loop(NB // UNROLL, PMAX // UNROLL, steps, 0)
    for u in range(UNROLL):
        apply(PMAX // UNROLL - 1, u)

    def blocks(parts):
        out = jnp.zeros((2 * NB, BLK * len(parts)), F32)
        for which, ref in ((0, con_t), (1, con_s)):
            x = jnp.concatenate([ref[c].reshape(PMAX, BLK) for c in parts], 1)
            for y in split(x, 2):
                out = out + jnp.dot(onehot[which], y.astype(BF16), preferred_element_type=F32)
        return out

    first = blocks((0,))
    near0[...] = first
    move0 = [
        send(near0.at[pl.ds(0, NB)], got_next3, 13, before3),
        send(near0, got_next2, 14, before2),
        send(near0, got_next, 15, before),
        send(near0.at[pl.ds(NB, NB)], got_prev, 16, after),
    ]
    others = blocks((1, 2))
    near12[0] = others[:NB, :BLK]
    near12[1] = others[:NB, BLK:]
    move12 = send(near12, got12, 17, before)

    element = (
        lax.broadcasted_iota(jnp.int32, (NB, BLK), 0) * BLK
        + lax.broadcasted_iota(jnp.int32, (NB, BLK), 1)
    )
    iota_lane = lax.broadcasted_iota(jnp.int32, (BLK, BLK), 1).astype(F32)
    hot_first = (0, NB, 3 * NB)
    hot_rows = ((NB, 2 * NB), (0, 2 * NB), (0, NB))
    part_row, part_lane, inside = [], [], []
    for copy in early:
        copy.wait_recv()
    for e in range(3):
        partner = element + offs[e]
        part_row.append(partner >> 7)
        part_lane.append(partner & 127)
        if e == 0:
            kept = me > 0
        else:
            kept = (me < devices - e) | (partner < NB * BLK)
        inside.append(jnp.where(kept, 0.5, 0.0).astype(F32))
        begin, end = hot_rows[e]
        iota_row = lax.broadcasted_iota(jnp.int32, (end - begin, BLK), 0) + begin
        upright_lane = part_lane[e].astype(F32).T
        for k in range(NB):
            lane = pl.ds(k * BLK, BLK)
            lanes_hot[e, lane, :] = jnp.where(
                iota_lane == upright_lane[:, k : k + 1], 1.0, 0.0
            ).astype(BF16)
            rows_hot[hot_first[e] : hot_first[e] + end - begin, lane] = jnp.where(
                iota_row == part_row[e][k : k + 1], 1.0, 0.0
            ).astype(BF16)

    def gather(ref, e):
        out = []
        for v in range(NB // 8):
            lane = part_lane[e][8 * v : 8 * v + 8]
            hot = part_row[e][8 * v : 8 * v + 8]
            acc = jnp.zeros((8, BLK), F32)
            for h in range(8 * v, 8 * v + 8 + NB):
                line = jnp.broadcast_to(ref[NB * e + h : NB * e + h + 1, :], (8, BLK))
                got = jnp.take_along_axis(line, lane, axis=1, mode="promise_in_bounds")
                acc = jnp.where(hot == h, got, acc)
            out.append(acc)
        return jnp.concatenate(out, 0)

    def scatter(flux, e):
        size = hot_rows[e][1] - hot_rows[e][0]
        hot_at = hot_first[e]
        at = 2 * hot_at
        top, rest = split(flux, 2)
        for k in range(NB):
            lane = pl.ds(k * BLK, BLK)
            hot = rows_hot[hot_at : hot_at + size, lane]
            for first_row, x in ((at, top), (at + size, rest)):
                line = jnp.broadcast_to(x[k : k + 1], (16, BLK)).astype(BF16)
                line = jnp.concatenate([line] * (size // 16), 0)
                spread[first_row : first_row + size, lane] = hot * line
        both = jnp.dot(spread[at : at + 2 * size, :], lanes_hot[e], preferred_element_type=F32)
        return both[:size] + both[size:]

    vecs = [table_inj[NB * e : NB * (e + 1), :] for e in range(3)]
    diffs = [vecs[e] - gather(table_inj, e) for e in range(3)]
    vec, sto = vecs[1], stores[0]

    def cubed(scale, t):
        aperture = scale * (1.0 + 0.5 * jnp.tanh(t))
        return aperture * aperture * aperture

    for copy in move0:
        copy.wait_recv()
    traction0 = first[NB:] + got_next[:NB, :]
    cubes = [
        cubed(bases[0], got_prev[...] + first[:NB]),
        cubed(bases[1], traction0),
        cubed(bases[2], got_next[NB:, :] + got_next2[:NB, :]),
        cubed(bases[3], got_next2[NB:, :] + got_next3[...]),
    ]
    for e in range(4):
        table[NB * e : NB * (e + 1), :] = cubes[e]
    weights = [inside[e] * (cubes[e] + gather(table, e)) for e in range(3)]
    weight = weights[1]
    fluxes = [weights[e] * diffs[e] for e in range(3)]
    landed = [scatter(fluxes[e], e) for e in range(3)]
    q = sto * vec + fluxes[1] - landed[1][:NB] - landed[0]
    q_next = stores[1] * vecs[2] + fluxes[2] - landed[2] - landed[1][NB:]
    table[NB : 2 * NB, :] = q
    table[2 * NB : 3 * NB, :] = q_next
    q_diff = q - gather(table, 1)
    flux = weight * q_diff

    def line(x):
        return jnp.sum(x, axis=0, keepdims=True)

    rows = [line(vec * vec), line(vec * q), line(q * q), line(sto * q * q + flux * q_diff)]
    sums = jnp.concatenate(rows + [jnp.zeros((4, BLK), F32)], 0)

    def distance(stage, j):
        if stage == 0:
            wide, narrow, far = low_size, core_size, j // core_size
        else:
            wide, narrow, far = high_size, x_size, j // x_size
        near = j % narrow
        return min(far, wide - far) + min(near, narrow - near)

    def exchange(stage, sums, got):
        sums_out[stage] = sums
        order = sorted(range(1, groups[stage]), key=functools.partial(distance, stage))
        for j in order[::-1]:
            pltpu.make_async_remote_copy(
                src_ref=sums_out.at[stage],
                dst_ref=got.at[j - 1],
                send_sem=red_send.at[stage],
                recv_sem=red_recv.at[stage],
                device_id=mate(stage, j),
                device_id_type=MESH,
            ).start()

    def collect(stage, sums, got):
        pltpu.make_async_copy(got, got, red_recv.at[stage]).wait()
        parts = [sums] + [got[j] for j in range(groups[stage] - 1)]
        while len(parts) > 1:
            parts = [sum(parts[j : j + 2]) for j in range(0, len(parts), 2)]
        return parts[0]

    exchange(0, sums, sums_near)
    landed = scatter(flux, 1)
    landed_out[...] = landed[NB:]
    move_u = send(landed_out, landed_in, 18, after)
    u_part = sto * q + flux - landed[:NB]
    sums = collect(0, sums, sums_near)
    exchange(1, sums, sums_far)
    move12.wait_recv()
    full = [
        traction0,
        others[NB:, :BLK] + got12[0],
        others[NB:, BLK:] + got12[1],
    ]
    for k in range(NB):
        rows = [x[k : k + 1] for x in full]
        traction[:, pl.ds(k * BLK, BLK)] = jnp.concatenate(rows, 0)
    move_u.wait_recv()
    u = u_part - landed_in[...]
    sums = collect(1, sums, sums_far)

    total = jnp.sum(sums, axis=1, keepdims=True)
    rr0, r0q, qq, qu = (total[j : j + 1] for j in range(4))
    alpha0 = rr0 / r0q
    rr1 = alpha0 * alpha0 * qq - rr0
    beta = rr1 / rr0
    alpha1 = rr1 / (r0q - 2.0 * alpha0 * qq + alpha0 * alpha0 * qu - beta * rr1 / alpha0)
    keep = 1.0 + beta
    r1 = vec - alpha0 * q
    residual[...] = r1 - alpha1 * (keep * q - alpha0 * u)
    pressure[...] = alpha0 * vec + alpha1 * (r1 + beta * vec)

    for copy in frame + early + move0 + [move12, move_u]:
        copy.wait_send()
    pltpu.make_async_copy(sums_near, sums_near, red_send.at[0]).wait()
    pltpu.make_async_copy(sums_far, sums_far, red_send.at[1]).wait()


def deliver(traction_in, pressure_in, residual_in, traction, pressure, residual, sem):
    refs = ((traction_in, traction), (pressure_in, pressure), (residual_in, residual))
    copies = [pltpu.make_async_copy(a, b, sem.at[j]) for j, (a, b) in enumerate(refs)]
    for copy in copies:
        copy.start()
    for copy in copies:
        copy.wait()


def shards(
    grp_size,
    seg_size,
    positions,
    normals,
    scales,
    displacement,
    pair_list,
    pair_count,
    base_aperture,
    storage,
    injection,
    link_offset,
):
    low_size = 8 if seg_size % 8 == 0 else 2
    high_size = seg_size // low_size
    sizes = (grp_size // 2, 2, high_size, low_size)
    square = (NB, BLK)
    vmem = pl.BlockSpec(memory_space=pltpu.VMEM)
    anywhere = pl.BlockSpec(memory_space=pl.ANY)
    rows3 = pltpu.VMEM((3, NB * BLK), F32)
    tile = pltpu.VMEM(square, F32)
    double = pltpu.VMEM((2 * NB, BLK), F32)
    scratch = [
        rows3,
        rows3,
        tile,
        rows3,
        pltpu.SMEM((2, PMAX), jnp.int32),
        pltpu.VMEM((2, PMAX), jnp.int32),
        pltpu.SMEM((1,), jnp.int32),
        pltpu.VMEM((4, NB, BLK), F32),
        pltpu.VMEM((2, NB, BLK), F32),
        pltpu.VMEM((3, NB, BLK), jnp.int32),
        rows3,
        rows3,
        tile,
        rows3,
        pltpu.VMEM((4 * NB, BLK), F32),
        pltpu.VMEM((NB, BLK, 48), BF16),
        pltpu.VMEM((2 * NB, 48, 2 * BLK), BF16),
        pltpu.VMEM((2 * NB, 16, 2 * BLK), BF16),
        pltpu.VMEM((NB, 3, BLK, BLK), F32),
        pltpu.VMEM((UNROLL, BLK, 2 * BLK), BF16),
        pltpu.VMEM((3, PMAX // 8, 8, BLK), F32),
        pltpu.VMEM((3, PMAX // 8, 8, BLK), F32),
        double,
        pltpu.VMEM((2, NB, BLK), F32),
        tile,
        double,
        double,
        tile,
        pltpu.VMEM((2, NB, BLK), F32),
        pltpu.VMEM((2, 2 * NB, PMAX), BF16),
        pltpu.VMEM((3, NB * BLK, BLK), BF16),
        pltpu.VMEM((4 * NB, NB * BLK), BF16),
        pltpu.VMEM((8 * NB, NB * BLK), BF16),
        pltpu.VMEM((4 * NB, BLK), F32),
        tile,
        tile,
        pltpu.VMEM((2, 8, BLK), F32),
        pltpu.VMEM((2 * low_size - 1, 8, BLK), F32),
        pltpu.VMEM((grp_size // 2 * high_size - 1, 8, BLK), F32),
        pltpu.SemaphoreType.DMA((19,)),
        pltpu.SemaphoreType.DMA((19,)),
        pltpu.SemaphoreType.DMA((2,)),
        pltpu.SemaphoreType.DMA((2,)),
        pltpu.SemaphoreType.DMA((11,)),
    ]
    shapes = (
        jax.ShapeDtypeStruct((3, NB * BLK), F32),
        jax.ShapeDtypeStruct(square, F32),
        jax.ShapeDtypeStruct(square, F32),
    )
    outs = pl.pallas_call(
        functools.partial(kernel, sizes),
        out_shape=shapes,
        in_specs=[anywhere] * 10,
        out_specs=(vmem, vmem, vmem),
        scratch_shapes=scratch,
        compiler_params=pltpu.CompilerParams(
            collective_id=0, has_side_effects=True, vmem_limit_bytes=56 << 20
        ),
        name="network",
    )(
        positions,
        normals,
        scales.reshape(square),
        displacement,
        pair_list,
        pair_count,
        base_aperture.reshape(square),
        storage.reshape(square),
        injection.reshape(square),
        link_offset.reshape(square),
    )
    traction, pressure, residual = pl.pallas_call(
        deliver,
        out_shape=shapes,
        in_specs=[vmem] * 3,
        out_specs=(anywhere,) * 3,
        scratch_shapes=[pltpu.SemaphoreType.DMA((3,))],
        name="deliver",
    )(*outs)
    return traction, pressure.reshape(-1), residual.reshape(-1)


def solution(mesh):
    return jax.shard_map(
        functools.partial(shards, mesh.shape["grp"], mesh.shape["seg"]),
        mesh=mesh,
        in_specs=(
            P(None, ("grp", "seg")),
            P(None, ("grp", "seg")),
            P(("grp", "seg")),
            P(None, ("grp", "seg")),
            P(None, ("grp", "seg")),
            P(("grp", "seg")),
            P(("grp", "seg")),
            P(("grp", "seg")),
            P(("grp", "seg")),
            P(("grp", "seg")),
        ),
        out_specs=(P(None, ("grp", "seg")), P(("grp", "seg")), P(("grp", "seg"))),
        check_vma=False,
    )
```

```python
import functools

import jax
import jax.numpy as jnp
from jax import lax
from jax.experimental import pallas as pl
from jax.experimental.pallas import tpu as pltpu
from jax.sharding import PartitionSpec as P

BLK = 128
NB = 32
PMAX = 160
F32 = jnp.float32
BF16 = jnp.bfloat16
MESH = pl.DeviceIdType.MESH
NT = (((1,), (1,)), ((), ()))
UNROLL = 16


def split(x, parts):
    out = []
    for _ in range(parts - 1):
        top = x.astype(BF16).astype(F32)
        out.append(top)
        x = x - top
    return out + [x]


def quads(vec, last):
    return jnp.concatenate([vec, last, vec, last], 0)


def kernel(
    sizes,
    pos_in,
    nrm_in,
    scl_in,
    dsp_in,
    pair_in,
    count_in,
    base_in,
    sto_in,
    inj_in,
    off_in,
    traction,
    pressure,
    residual,
    pos,
    nrm,
    scl,
    dsp,
    pairs,
    pair_rows,
    count,
    bases,
    stores,
    offs,
    prev_pos,
    prev_nrm,
    prev_scl,
    prev_dsp,
    table_inj,
    tfeat,
    sfeat,
    dfeat,
    columns,
    held,
    con_t,
    con_s,
    near0,
    near12,
    got_prev,
    got_next,
    got_next2,
    got_next3,
    got12,
    onehot,
    lanes_hot,
    rows_hot,
    spread,
    table,
    landed_out,
    landed_in,
    sums_out,
    sums_near,
    sums_far,
    send_sem,
    recv_sem,
    red_send,
    red_recv,
    load_sem,
):
    x_size, core_size, high_size, low_size = sizes
    grp_size, seg_size = x_size * core_size, high_size * low_size
    devices = grp_size * seg_size
    grp = lax.axis_index("grp")
    seg = lax.axis_index("seg")
    me = grp * seg_size + seg

    def device(shift):
        to = lax.rem(me + shift + devices, devices)
        return (to // seg_size, lax.rem(to, seg_size))

    def ring(index, size, low, shift):
        digit = index // low
        if size * low > 1:
            digit = lax.rem(digit, size)
        return index + (lax.rem(digit + shift, size) - digit) * low

    groups = (core_size * low_size, x_size * high_size)
    rings = (
        (
            [ring(grp, core_size, 1, j) for j in range(core_size)],
            [ring(seg, low_size, 1, j) for j in range(low_size)],
        ),
        (
            [ring(grp, x_size, core_size, j) for j in range(x_size)],
            [ring(seg, high_size, low_size, j) for j in range(high_size)],
        ),
    )

    def mate(stage, j):
        narrow, wide = rings[stage]
        return (narrow[j % len(narrow)], wide[j // len(narrow)])

    def distance(stage, j):
        narrow, wide = (len(x) for x in rings[stage])
        near, far = j % narrow, j // narrow
        return min(far, wide - far) + min(near, narrow - near)

    orders = [
        sorted(range(1, groups[stage]), key=functools.partial(distance, stage))[::-1]
        for stage in (0, 1)
    ]

    def start_load(slot, src, dst):
        load = pltpu.make_async_copy(src, dst, load_sem.at[slot])
        load.start()
        return load

    loads = [
        start_load(0, pos_in, pos),
        start_load(1, nrm_in, nrm),
        start_load(2, scl_in, scl),
        start_load(3, dsp_in, dsp),
    ]
    mates = [mate(stage, j) for stage in (1, 0) for j in orders[stage]]
    mates += [device(shift) for shift in (3, -3, 2, -2, 1, -1)]
    barrier = pltpu.get_barrier_semaphore()
    for to in mates:
        pl.semaphore_signal(barrier, inc=1, device_id=to, device_id_type=MESH)
    loads += [
        start_load(4, pair_in, pairs),
        start_load(5, pair_in, pair_rows),
        start_load(6, count_in, count),
        start_load(7, inj_in, table_inj.at[pl.ds(NB, NB)]),
        start_load(8, off_in, offs.at[1]),
        start_load(9, base_in, bases.at[1]),
        start_load(10, sto_in, stores.at[0]),
    ]
    pl.semaphore_wait(barrier, len(mates))

    def send(src, dst, slot, to):
        copy = pltpu.make_async_remote_copy(
            src_ref=src,
            dst_ref=dst,
            send_sem=send_sem.at[slot],
            recv_sem=recv_sem.at[slot],
            device_id=to,
            device_id_type=MESH,
        )
        copy.start()
        return copy

    after, before, before2, before3 = (device(shift) for shift in (1, -1, -2, -3))
    frame = [
        send(pos_in, prev_pos, 0, after),
        send(nrm_in, prev_nrm, 1, after),
        send(scl_in, prev_scl, 2, after),
        send(dsp_in, prev_dsp, 3, after),
    ]
    early = [
        send(inj_in, table_inj.at[pl.ds(2 * NB, NB)], 4, before),
        send(off_in, offs.at[2], 5, before),
        send(base_in, bases.at[2], 6, before),
        send(sto_in, stores.at[1], 7, before),
        send(inj_in, table_inj.at[pl.ds(3 * NB, NB)], 8, before2),
        send(base_in, bases.at[3], 9, before2),
    ]
    for slot in range(4):
        loads[slot].wait()

    row = lax.broadcasted_iota(jnp.int32, (8, BLK), 0)
    low4 = row < 4
    is3 = row == 3
    is7 = row == 7
    is_norm = is3 | is7
    zeros8 = jnp.zeros((8, BLK), F32)
    centre = jnp.mean(pos[...], axis=1, keepdims=True)

    def target_block(k):
        lane = pl.ds(pl.multiple_of(k * BLK, BLK), BLK)
        p = pos[:, lane] - centre
        q = quads(p, jnp.sum(p * p, axis=0, keepdims=True))
        q1, q2, q3 = split(jnp.where(is_norm, q, -2.0 * q), 3)
        s = scl[pl.ds(k, 1), :]
        r = quads(nrm[:, lane] * s * 0.125, 0.25 * s)
        r1, r2, r3 = split(r, 3)
        rows = [
            jnp.where(is7, 1.0, q1),
            jnp.where(is7, 1.0, q2),
            jnp.where(is7, 1.0, jnp.where(low4, q3, q1)),
            r1,
            r2,
            jnp.where(low4, r3, r1),
        ]
        d = dsp[:, lane]
        rows += [jnp.concatenate([d, jnp.zeros((5, BLK), F32)], 0)]
        upright = jnp.concatenate(rows, 0).T
        tfeat[k] = upright[:, :48].astype(BF16)
        for c in range(3):
            columns[k, c] = jnp.broadcast_to(upright[:, 48 + c : 49 + c], (BLK, BLK))

    def source_block(pos_ref, nrm_ref, scl_ref, first, factor, k):
        lane = pl.ds(pl.multiple_of(k * BLK, BLK), BLK)
        p = pos_ref[:, lane] - centre
        q1, q2, q3 = split(quads(p, jnp.sum(p * p, axis=0, keepdims=True) + 0.25), 3)
        s = scl_ref[pl.ds(k, 1), :]
        if factor is not None:
            s = jnp.where(factor, s, 0.0)
        r1, r2, r3 = split(quads(nrm_ref[:, lane] * s, s), 3)
        ahead = [
            jnp.where(is3, 1.0, jnp.where(is7 | low4, q1, q2)),
            jnp.where(is3, 1.0, jnp.where(low4, q1, q2)),
            jnp.where(is3, 1.0, jnp.where(low4, q1, q3)),
            zeros8,
            zeros8,
            zeros8,
        ]
        align = [
            zeros8,
            zeros8,
            zeros8,
            jnp.where(low4, r1, r2),
            jnp.where(low4, r1, r2),
            jnp.where(low4, r1, r3),
        ]
        sfeat[first + k, :, :BLK] = jnp.concatenate(ahead, 0).astype(BF16)
        sfeat[first + k, :, BLK:] = jnp.concatenate(align, 0).astype(BF16)

    def moved_block(dsp_ref, first, k):
        lane = pl.ds(pl.multiple_of(k * BLK, BLK), BLK)
        d = dsp_ref[:, lane]
        d1, d2 = split(quads(d, jnp.zeros((1, BLK), F32)), 2)
        both = jnp.concatenate([jnp.where(low4, d1, d2), zeros8], 0).astype(BF16)
        dfeat[first + k, :, :BLK] = both
        dfeat[first + k, :, BLK:] = both

    def own_blocks(i, _):
        for j in range(4):
            target_block(4 * i + j)
            source_block(pos, nrm, scl, NB, None, 4 * i + j)
            moved_block(dsp, NB, 4 * i + j)
        return 0

    def prev_blocks(i, _):
        for j in range(8):
            source_block(prev_pos, prev_nrm, prev_scl, 0, me > 0, 8 * i + j)
        return 0

    def prev_moved(i, _):
        for j in range(8):
            moved_block(prev_dsp, 0, 8 * i + j)
        return 0

    lax.fori_loop(0, NB // 4, own_blocks, 0)

    for slot in range(4, 11):
        loads[slot].wait()

    slot = lax.broadcasted_iota(jnp.int32, (2 * NB, PMAX), 1)
    block = lax.broadcasted_iota(jnp.int32, (2 * NB, PMAX), 0)
    tgt = pair_rows[0:1, :] + NB
    src = pair_rows[1:2, :]
    live = slot < count[0]
    onehot[0] = jnp.where(live & (block == tgt), 1.0, 0.0).astype(BF16)
    onehot[1] = jnp.where(live & (block == src) & (src != tgt), 1.0, 0.0).astype(BF16)

    def apply(i, u):
        s = pairs[1, i * UNROLL + u]
        out = lax.dot_general(dfeat[s], held[u], NT, preferred_element_type=F32)
        out = out[:4] + out[4:8]
        for c in range(3):
            con_t[c, i * (UNROLL // 8) + u // 8, u % 8 : u % 8 + 1, :] = out[c : c + 1]

    def evaluate(i, u):
        p = i * UNROLL + u
        t = pairs[0, p]
        m = jnp.dot(tfeat[t], sfeat[pairs[1, p]], preferred_element_type=F32)
        g = m[:, BLK:] * lax.rsqrt(m[:, :BLK])
        top = g.astype(BF16)
        held[u, :, :BLK] = top
        held[u, :, BLK:] = (g - top.astype(F32)).astype(BF16)
        for c in range(3):
            con_s[c, i * (UNROLL // 8) + u // 8, u % 8 : u % 8 + 1, :] = jnp.sum(
                g * columns[t, c], axis=0, keepdims=True
            )

    def steps(i, _):
        for u in range(UNROLL):
            apply(i - 1, u)
            evaluate(i, u)
        return 0

    for u in range(UNROLL):
        evaluate(0, u)
    lax.fori_loop(1, NB // UNROLL, steps, 0)
    for copy in frame[:3]:
        copy.wait_recv()
    early += [
        send(inj_in, table_inj.at[pl.ds(0, NB)], 10, after),
        send(off_in, offs.at[0], 11, after),
        send(base_in, bases.at[0], 12, after),
    ]
    lax.fori_loop(0, NB // 8, prev_blocks, 0)
    frame[3].wait_recv()
    lax.fori_loop(0, NB // 8, prev_moved, 0)
    lax.fori_loop(NB // UNROLL, PMAX // UNROLL, steps, 0)
    for u in range(UNROLL):
        apply(PMAX // UNROLL - 1, u)

    def blocks(parts):
        out = jnp.zeros((2 * NB, BLK * len(parts)), F32)
        for which, ref in ((0, con_t), (1, con_s)):
            x = jnp.concatenate([ref[c].reshape(PMAX, BLK) for c in parts], 1)
            for y in split(x, 2):
                out = out + jnp.dot(onehot[which], y.astype(BF16), preferred_element_type=F32)
        return out

    first = blocks((0,))
    near0[...] = first
    move0 = [
        send(near0.at[pl.ds(0, NB)], got_next3, 13, before3),
        send(near0, got_next2, 14, before2),
        send(near0, got_next, 15, before),
        send(near0.at[pl.ds(NB, NB)], got_prev, 16, after),
    ]
    others = blocks((1, 2))
    near12[0] = others[:NB, :BLK]
    near12[1] = others[:NB, BLK:]
    move12 = send(near12, got12, 17, before)

    element = (
        lax.broadcasted_iota(jnp.int32, (NB, BLK), 0) * BLK
        + lax.broadcasted_iota(jnp.int32, (NB, BLK), 1)
    )
    iota_lane = lax.broadcasted_iota(jnp.int32, (BLK, BLK), 1).astype(F32)
    hot_first = (0, NB, 3 * NB)
    hot_rows = ((NB, 2 * NB), (0, 2 * NB), (0, NB))
    part_row, part_lane, inside = [], [], []
    for copy in early:
        copy.wait_recv()
    for e in range(3):
        partner = element + offs[e]
        part_row.append(partner >> 7)
        part_lane.append(partner & 127)
        if e == 0:
            kept = me > 0
        else:
            kept = (me < devices - e) | (partner < NB * BLK)
        inside.append(jnp.where(kept, 0.5, 0.0).astype(F32))
        begin, end = hot_rows[e]
        iota_row = lax.broadcasted_iota(jnp.int32, (end - begin, BLK), 0) + begin
        upright_lane = part_lane[e].astype(F32).T
        for k in range(NB):
            lane = pl.ds(k * BLK, BLK)
            lanes_hot[e, lane, :] = jnp.where(
                iota_lane == upright_lane[:, k : k + 1], 1.0, 0.0
            ).astype(BF16)
            rows_hot[hot_first[e] : hot_first[e] + end - begin, lane] = jnp.where(
                iota_row == part_row[e][k : k + 1], 1.0, 0.0
            ).astype(BF16)

    def gather(ref, e):
        out = []
        for v in range(NB // 8):
            lane = part_lane[e][8 * v : 8 * v + 8]
            hot = part_row[e][8 * v : 8 * v + 8]
            acc = jnp.zeros((8, BLK), F32)
            for h in range(max(8 * v, hot_rows[e][0]), 8 * v + 8 + NB):
                line = jnp.broadcast_to(ref[NB * e + h : NB * e + h + 1, :], (8, BLK))
                got = jnp.take_along_axis(line, lane, axis=1, mode="promise_in_bounds")
                acc = jnp.where(hot == h, got, acc)
            out.append(acc)
        return jnp.concatenate(out, 0)

    def scatter(flux, e):
        size = hot_rows[e][1] - hot_rows[e][0]
        hot_at = hot_first[e]
        at = 2 * hot_at
        top, rest = split(flux, 2)
        for k in range(NB):
            lane = pl.ds(k * BLK, BLK)
            hot = rows_hot[hot_at : hot_at + size, lane]
            for first_row, x in ((at, top), (at + size, rest)):
                line = jnp.broadcast_to(x[k : k + 1], (16, BLK)).astype(BF16)
                line = jnp.concatenate([line] * (size // 16), 0)
                spread[first_row : first_row + size, lane] = hot * line
        both = jnp.dot(spread[at : at + 2 * size, :], lanes_hot[e], preferred_element_type=F32)
        return both[:size] + both[size:]

    vecs = [table_inj[NB * e : NB * (e + 1), :] for e in range(3)]
    diffs = [vecs[e] - gather(table_inj, e) for e in range(3)]
    vec, sto = vecs[1], stores[0]

    def cubed(scale, t):
        aperture = scale * (1.0 + 0.5 * jnp.tanh(t))
        return aperture * aperture * aperture

    for copy in move0:
        copy.wait_recv()
    traction0 = first[NB:] + got_next[:NB, :]
    cubes = [
        cubed(bases[0], got_prev[...] + first[:NB]),
        cubed(bases[1], traction0),
        cubed(bases[2], got_next[NB:, :] + got_next2[:NB, :]),
        cubed(bases[3], got_next2[NB:, :] + got_next3[...]),
    ]
    for e in range(4):
        table[NB * e : NB * (e + 1), :] = cubes[e]
    weights = [inside[e] * (cubes[e] + gather(table, e)) for e in range(3)]
    weight = weights[1]
    fluxes = [weights[e] * diffs[e] for e in range(3)]
    landed = [scatter(fluxes[e], e) for e in range(3)]
    q = sto * vec + fluxes[1] - landed[1][:NB] - landed[0]
    q_next = stores[1] * vecs[2] + fluxes[2] - landed[2] - landed[1][NB:]
    table[NB : 2 * NB, :] = q
    table[2 * NB : 3 * NB, :] = q_next
    q_diff = q - gather(table, 1)
    flux = weight * q_diff

    def line(x):
        return jnp.sum(x, axis=0, keepdims=True)

    rows = [line(vec * vec), line(vec * q), line(q * q), line(sto * q * q + flux * q_diff)]
    sums = jnp.concatenate(rows + [jnp.zeros((4, BLK), F32)], 0)

    def exchange(stage, sums, got):
        sums_out[stage] = sums
        for j in orders[stage]:
            pltpu.make_async_remote_copy(
                src_ref=sums_out.at[stage],
                dst_ref=got.at[j - 1],
                send_sem=red_send.at[stage],
                recv_sem=red_recv.at[stage],
                device_id=mate(stage, j),
                device_id_type=MESH,
            ).start()

    def collect(stage, sums, got):
        pltpu.make_async_copy(got, got, red_recv.at[stage]).wait()
        parts = [sums] + [got[j] for j in range(groups[stage] - 1)]
        while len(parts) > 1:
            parts = [sum(parts[j : j + 2]) for j in range(0, len(parts), 2)]
        return parts[0]

    exchange(0, sums, sums_near)
    landed = scatter(flux, 1)
    landed_out[...] = landed[NB:]
    move_u = send(landed_out, landed_in, 18, after)
    u_part = sto * q + flux - landed[:NB]
    sums = collect(0, sums, sums_near)
    exchange(1, sums, sums_far)
    move12.wait_recv()
    full = [
        traction0,
        others[NB:, :BLK] + got12[0],
        others[NB:, BLK:] + got12[1],
    ]
    for k in range(NB):
        rows = [x[k : k + 1] for x in full]
        traction[:, pl.ds(k * BLK, BLK)] = jnp.concatenate(rows, 0)
    move_u.wait_recv()
    u = u_part - landed_in[...]
    sums = collect(1, sums, sums_far)

    total = jnp.sum(sums, axis=1, keepdims=True)
    rr0, r0q, qq, qu = (total[j : j + 1] for j in range(4))
    alpha0 = rr0 / r0q
    rr1 = alpha0 * alpha0 * qq - rr0
    beta = rr1 / rr0
    alpha1 = rr1 / (r0q - 2.0 * alpha0 * qq + alpha0 * alpha0 * qu - beta * rr1 / alpha0)
    keep = 1.0 + beta
    r1 = vec - alpha0 * q
    residual[...] = r1 - alpha1 * (keep * q - alpha0 * u)
    pressure[...] = alpha0 * vec + alpha1 * (r1 + beta * vec)

    for copy in frame + early + move0 + [move12, move_u]:
        copy.wait_send()
    pltpu.make_async_copy(sums_near, sums_near, red_send.at[0]).wait()
    pltpu.make_async_copy(sums_far, sums_far, red_send.at[1]).wait()


def deliver(traction_in, pressure_in, residual_in, traction, pressure, residual, sem):
    refs = ((traction_in, traction), (pressure_in, pressure), (residual_in, residual))
    copies = [pltpu.make_async_copy(a, b, sem.at[j]) for j, (a, b) in enumerate(refs)]
    for copy in copies:
        copy.start()
    for copy in copies:
        copy.wait()


def shards(
    grp_size,
    seg_size,
    positions,
    normals,
    scales,
    displacement,
    pair_list,
    pair_count,
    base_aperture,
    storage,
    injection,
    link_offset,
):
    low_size = 8 if seg_size % 8 == 0 else 2
    high_size = seg_size // low_size
    sizes = (grp_size // 2, 2, high_size, low_size)
    square = (NB, BLK)
    vmem = pl.BlockSpec(memory_space=pltpu.VMEM)
    anywhere = pl.BlockSpec(memory_space=pl.ANY)
    rows3 = pltpu.VMEM((3, NB * BLK), F32)
    tile = pltpu.VMEM(square, F32)
    double = pltpu.VMEM((2 * NB, BLK), F32)
    scratch = [
        rows3,
        rows3,
        tile,
        rows3,
        pltpu.SMEM((2, PMAX), jnp.int32),
        pltpu.VMEM((2, PMAX), jnp.int32),
        pltpu.SMEM((1,), jnp.int32),
        pltpu.VMEM((4, NB, BLK), F32),
        pltpu.VMEM((2, NB, BLK), F32),
        pltpu.VMEM((3, NB, BLK), jnp.int32),
        rows3,
        rows3,
        tile,
        rows3,
        pltpu.VMEM((4 * NB, BLK), F32),
        pltpu.VMEM((NB, BLK, 48), BF16),
        pltpu.VMEM((2 * NB, 48, 2 * BLK), BF16),
        pltpu.VMEM((2 * NB, 16, 2 * BLK), BF16),
        pltpu.VMEM((NB, 3, BLK, BLK), F32),
        pltpu.VMEM((UNROLL, BLK, 2 * BLK), BF16),
        pltpu.VMEM((3, PMAX // 8, 8, BLK), F32),
        pltpu.VMEM((3, PMAX // 8, 8, BLK), F32),
        double,
        pltpu.VMEM((2, NB, BLK), F32),
        tile,
        double,
        double,
        tile,
        pltpu.VMEM((2, NB, BLK), F32),
        pltpu.VMEM((2, 2 * NB, PMAX), BF16),
        pltpu.VMEM((3, NB * BLK, BLK), BF16),
        pltpu.VMEM((4 * NB, NB * BLK), BF16),
        pltpu.VMEM((8 * NB, NB * BLK), BF16),
        pltpu.VMEM((4 * NB, BLK), F32),
        tile,
        tile,
        pltpu.VMEM((2, 8, BLK), F32),
        pltpu.VMEM((2 * low_size - 1, 8, BLK), F32),
        pltpu.VMEM((grp_size // 2 * high_size - 1, 8, BLK), F32),
        pltpu.SemaphoreType.DMA((19,)),
        pltpu.SemaphoreType.DMA((19,)),
        pltpu.SemaphoreType.DMA((2,)),
        pltpu.SemaphoreType.DMA((2,)),
        pltpu.SemaphoreType.DMA((11,)),
    ]
    shapes = (
        jax.ShapeDtypeStruct((3, NB * BLK), F32),
        jax.ShapeDtypeStruct(square, F32),
        jax.ShapeDtypeStruct(square, F32),
    )
    outs = pl.pallas_call(
        functools.partial(kernel, sizes),
        out_shape=shapes,
        in_specs=[anywhere] * 10,
        out_specs=(vmem, vmem, vmem),
        scratch_shapes=scratch,
        compiler_params=pltpu.CompilerParams(
            collective_id=0, has_side_effects=True, vmem_limit_bytes=56 << 20
        ),
        name="network",
    )(
        positions,
        normals,
        scales.reshape(square),
        displacement,
        pair_list,
        pair_count,
        base_aperture.reshape(square),
        storage.reshape(square),
        injection.reshape(square),
        link_offset.reshape(square),
    )
    traction, pressure, residual = pl.pallas_call(
        deliver,
        out_shape=shapes,
        in_specs=[vmem] * 3,
        out_specs=(anywhere,) * 3,
        scratch_shapes=[pltpu.SemaphoreType.DMA((3,))],
        name="deliver",
    )(*outs)
    return traction, pressure.reshape(-1), residual.reshape(-1)


def solution(mesh):
    return jax.shard_map(
        functools.partial(shards, mesh.shape["grp"], mesh.shape["seg"]),
        mesh=mesh,
        in_specs=(
            P(None, ("grp", "seg")),
            P(None, ("grp", "seg")),
            P(("grp", "seg")),
            P(None, ("grp", "seg")),
            P(None, ("grp", "seg")),
            P(("grp", "seg")),
            P(("grp", "seg")),
            P(("grp", "seg")),
            P(("grp", "seg")),
            P(("grp", "seg")),
        ),
        out_specs=(P(None, ("grp", "seg")), P(("grp", "seg")), P(("grp", "seg"))),
        check_vma=False,
    )
```

```python
import functools

import jax
import jax.numpy as jnp
from jax import lax
from jax.experimental import pallas as pl
from jax.experimental.pallas import tpu as pltpu
from jax.sharding import PartitionSpec as P

BLK = 128
NB = 32
PMAX = 160
F32 = jnp.float32
BF16 = jnp.bfloat16
MESH = pl.DeviceIdType.MESH
NT = (((1,), (1,)), ((), ()))
UNROLL = 32


def split(x, parts):
    out = []
    for _ in range(parts - 1):
        top = x.astype(BF16).astype(F32)
        out.append(top)
        x = x - top
    return out + [x]


def quads(vec, last):
    return jnp.concatenate([vec, last, vec, last], 0)


def kernel(
    sizes,
    pos_in,
    nrm_in,
    scl_in,
    dsp_in,
    pair_in,
    count_in,
    base_in,
    sto_in,
    inj_in,
    off_in,
    traction,
    pressure,
    residual,
    pos,
    nrm,
    scl,
    dsp,
    pairs,
    pair_rows,
    count,
    bases,
    stores,
    offs,
    prev_pos,
    prev_nrm,
    prev_scl,
    prev_dsp,
    table_inj,
    tfeat,
    sfeat,
    dfeat,
    columns,
    held,
    con_t,
    con_s,
    near0,
    near12,
    got_prev,
    got_next,
    got_next2,
    got_next3,
    got12,
    onehot,
    lanes_hot,
    rows_hot,
    spread,
    table,
    landed_out,
    landed_in,
    sums_out,
    sums_near,
    sums_far,
    send_sem,
    recv_sem,
    red_send,
    red_recv,
    load_sem,
):
    x_size, core_size, high_size, low_size = sizes
    grp_size, seg_size = x_size * core_size, high_size * low_size
    devices = grp_size * seg_size
    grp = lax.axis_index("grp")
    seg = lax.axis_index("seg")
    me = grp * seg_size + seg

    def device(shift):
        to = lax.rem(me + shift + devices, devices)
        return (to // seg_size, lax.rem(to, seg_size))

    def ring(index, size, low, shift):
        digit = index // low
        if size * low > 1:
            digit = lax.rem(digit, size)
        return index + (lax.rem(digit + shift, size) - digit) * low

    groups = (core_size * low_size, x_size * high_size)
    rings = (
        (
            [ring(grp, core_size, 1, j) for j in range(core_size)],
            [ring(seg, low_size, 1, j) for j in range(low_size)],
        ),
        (
            [ring(grp, x_size, core_size, j) for j in range(x_size)],
            [ring(seg, high_size, low_size, j) for j in range(high_size)],
        ),
    )

    def mate(stage, j):
        narrow, wide = rings[stage]
        return (narrow[j % len(narrow)], wide[j // len(narrow)])

    def distance(stage, j):
        narrow, wide = (len(x) for x in rings[stage])
        near, far = j % narrow, j // narrow
        return min(far, wide - far) + min(near, narrow - near)

    orders = [
        sorted(range(1, groups[stage]), key=functools.partial(distance, stage))[::-1]
        for stage in (0, 1)
    ]

    def start_load(slot, src, dst):
        load = pltpu.make_async_copy(src, dst, load_sem.at[slot])
        load.start()
        return load

    loads = [
        start_load(0, pos_in, pos),
        start_load(1, nrm_in, nrm),
        start_load(2, scl_in, scl),
        start_load(3, dsp_in, dsp),
    ]
    mates = [mate(stage, j) for stage in (1, 0) for j in orders[stage]]
    mates += [device(shift) for shift in (3, -3, 2, -2, 1, -1)]
    barrier = pltpu.get_barrier_semaphore()
    for to in mates:
        pl.semaphore_signal(barrier, inc=1, device_id=to, device_id_type=MESH)
    loads += [
        start_load(4, pair_in, pairs),
        start_load(5, pair_in, pair_rows),
        start_load(6, count_in, count),
        start_load(7, inj_in, table_inj.at[pl.ds(NB, NB)]),
        start_load(8, off_in, offs.at[1]),
        start_load(9, base_in, bases.at[1]),
        start_load(10, sto_in, stores.at[0]),
    ]
    pl.semaphore_wait(barrier, len(mates))

    def send(src, dst, slot, to):
        copy = pltpu.make_async_remote_copy(
            src_ref=src,
            dst_ref=dst,
            send_sem=send_sem.at[slot],
            recv_sem=recv_sem.at[slot],
            device_id=to,
            device_id_type=MESH,
        )
        copy.start()
        return copy

    after, before, before2, before3 = (device(shift) for shift in (1, -1, -2, -3))
    frame = []
    for c in range(4):
        lanes = pl.ds(c * (NB // 4) * BLK, NB // 4 * BLK)
        rows = pl.ds(c * (NB // 4), NB // 4)
        frame.append(
            [
                send(pos_in.at[:, lanes], prev_pos.at[:, lanes], 19 + 3 * c, after),
                send(nrm_in.at[:, lanes], prev_nrm.at[:, lanes], 20 + 3 * c, after),
                send(scl_in.at[rows], prev_scl.at[rows], 21 + 3 * c, after),
            ]
        )
    frame_dsp = send(dsp_in, prev_dsp, 3, after)
    early = [
        send(inj_in, table_inj.at[pl.ds(2 * NB, NB)], 4, before),
        send(off_in, offs.at[2], 5, before),
        send(base_in, bases.at[2], 6, before),
        send(sto_in, stores.at[1], 7, before),
        send(inj_in, table_inj.at[pl.ds(3 * NB, NB)], 8, before2),
        send(base_in, bases.at[3], 9, before2),
    ]
    for slot in range(4):
        loads[slot].wait()

    row = lax.broadcasted_iota(jnp.int32, (8, BLK), 0)
    low4 = row < 4
    is3 = row == 3
    is7 = row == 7
    is_norm = is3 | is7
    zeros8 = jnp.zeros((8, BLK), F32)
    centre = jnp.mean(pos[...], axis=1, keepdims=True)

    def target_block(k):
        lane = pl.ds(pl.multiple_of(k * BLK, BLK), BLK)
        p = pos[:, lane] - centre
        q = quads(p, jnp.sum(p * p, axis=0, keepdims=True))
        q1, q2, q3 = split(jnp.where(is_norm, q, -2.0 * q), 3)
        s = scl[pl.ds(k, 1), :]
        r = quads(nrm[:, lane] * s * 0.125, 0.25 * s)
        r1, r2, r3 = split(r, 3)
        rows = [
            jnp.where(is7, 1.0, q1),
            jnp.where(is7, 1.0, q2),
            jnp.where(is7, 1.0, jnp.where(low4, q3, q1)),
            r1,
            r2,
            jnp.where(low4, r3, r1),
        ]
        d = dsp[:, lane]
        rows += [jnp.concatenate([d, jnp.zeros((5, BLK), F32)], 0)]
        upright = jnp.concatenate(rows, 0).T
        tfeat[k] = upright[:, :48].astype(BF16)
        for c in range(3):
            columns[k, c] = jnp.broadcast_to(upright[:, 48 + c : 49 + c], (BLK, BLK))

    def source_block(pos_ref, nrm_ref, scl_ref, first, factor, k):
        lane = pl.ds(pl.multiple_of(k * BLK, BLK), BLK)
        p = pos_ref[:, lane] - centre
        q1, q2, q3 = split(quads(p, jnp.sum(p * p, axis=0, keepdims=True) + 0.25), 3)
        s = scl_ref[pl.ds(k, 1), :]
        if factor is not None:
            s = jnp.where(factor, s, 0.0)
        r1, r2, r3 = split(quads(nrm_ref[:, lane] * s, s), 3)
        ahead = [
            jnp.where(is3, 1.0, jnp.where(is7 | low4, q1, q2)),
            jnp.where(is3, 1.0, jnp.where(low4, q1, q2)),
            jnp.where(is3, 1.0, jnp.where(low4, q1, q3)),
            zeros8,
            zeros8,
            zeros8,
        ]
        align = [
            zeros8,
            zeros8,
            zeros8,
            jnp.where(low4, r1, r2),
            jnp.where(low4, r1, r2),
            jnp.where(low4, r1, r3),
        ]
        sfeat[first + k, :, :BLK] = jnp.concatenate(ahead, 0).astype(BF16)
        sfeat[first + k, :, BLK:] = jnp.concatenate(align, 0).astype(BF16)

    def moved_block(dsp_ref, first, k):
        lane = pl.ds(pl.multiple_of(k * BLK, BLK), BLK)
        d = dsp_ref[:, lane]
        d1, d2 = split(quads(d, jnp.zeros((1, BLK), F32)), 2)
        both = jnp.concatenate([jnp.where(low4, d1, d2), zeros8], 0).astype(BF16)
        dfeat[first + k, :, :BLK] = both
        dfeat[first + k, :, BLK:] = both

    def own_blocks(i, _):
        for j in range(4):
            target_block(4 * i + j)
            source_block(pos, nrm, scl, NB, None, 4 * i + j)
            moved_block(dsp, NB, 4 * i + j)
        return 0

    def prev_moved(i, _):
        for j in range(8):
            moved_block(prev_dsp, 0, 8 * i + j)
        return 0

    lax.fori_loop(0, NB // 4, own_blocks, 0)

    for slot in range(4, 11):
        loads[slot].wait()

    slot = lax.broadcasted_iota(jnp.int32, (2 * NB, PMAX), 1)
    block = lax.broadcasted_iota(jnp.int32, (2 * NB, PMAX), 0)
    tgt = pair_rows[0:1, :] + NB
    src = pair_rows[1:2, :]
    live = slot < count[0]
    onehot[0] = jnp.where(live & (block == tgt), 1.0, 0.0).astype(BF16)
    onehot[1] = jnp.where(live & (block == src) & (src != tgt), 1.0, 0.0).astype(BF16)

    def apply(i, u):
        s = pairs[1, i * UNROLL + u]
        out = lax.dot_general(dfeat[s], held[u], NT, preferred_element_type=F32)
        out = out[:4] + out[4:8]
        for c in range(3):
            con_t[c, i * (UNROLL // 8) + u // 8, u % 8 : u % 8 + 1, :] = out[c : c + 1]

    def evaluate(i, u):
        p = i * UNROLL + u
        t = pairs[0, p]
        m = jnp.dot(tfeat[t], sfeat[pairs[1, p]], preferred_element_type=F32)
        g = m[:, BLK:] * lax.rsqrt(m[:, :BLK])
        top = g.astype(BF16)
        held[u, :, :BLK] = top
        held[u, :, BLK:] = (g - top.astype(F32)).astype(BF16)
        for c in range(3):
            con_s[c, i * (UNROLL // 8) + u // 8, u % 8 : u % 8 + 1, :] = jnp.sum(
                g * columns[t, c], axis=0, keepdims=True
            )

    def steps(i, _):
        for u in range(UNROLL):
            apply(i - 1, u)
            evaluate(i, u)
        return 0

    for u in range(UNROLL):
        evaluate(0, u)
    lax.fori_loop(1, NB // UNROLL, steps, 0)
    for c in range(4):
        for copy in frame[c]:
            copy.wait_recv()
        for j in range(NB // 4):
            source_block(prev_pos, prev_nrm, prev_scl, 0, me > 0, c * (NB // 4) + j)
    early += [
        send(inj_in, table_inj.at[pl.ds(0, NB)], 10, after),
        send(off_in, offs.at[0], 11, after),
        send(base_in, bases.at[0], 12, after),
    ]
    lax.fori_loop(NB // UNROLL, NB // UNROLL + 1, steps, 0)
    frame_dsp.wait_recv()
    lax.fori_loop(0, NB // 8, prev_moved, 0)
    lax.fori_loop(NB // UNROLL + 1, PMAX // UNROLL, steps, 0)
    for u in range(UNROLL):
        apply(PMAX // UNROLL - 1, u)

    def blocks(parts):
        out = jnp.zeros((2 * NB, BLK * len(parts)), F32)
        for which, ref in ((0, con_t), (1, con_s)):
            x = jnp.concatenate([ref[c].reshape(PMAX, BLK) for c in parts], 1)
            for y in split(x, 2):
                out = out + jnp.dot(onehot[which], y.astype(BF16), preferred_element_type=F32)
        return out

    first = blocks((0,))
    near0[...] = first
    move0 = [
        send(near0.at[pl.ds(0, NB)], got_next3, 13, before3),
        send(near0, got_next2, 14, before2),
        send(near0, got_next, 15, before),
        send(near0.at[pl.ds(NB, NB)], got_prev, 16, after),
    ]
    others = blocks((1, 2))
    near12[0] = others[:NB, :BLK]
    near12[1] = others[:NB, BLK:]
    move12 = send(near12, got12, 17, before)

    element = (
        lax.broadcasted_iota(jnp.int32, (NB, BLK), 0) * BLK
        + lax.broadcasted_iota(jnp.int32, (NB, BLK), 1)
    )
    iota_lane = lax.broadcasted_iota(jnp.int32, (BLK, BLK), 1).astype(F32)
    hot_first = (0, NB, 3 * NB)
    hot_rows = ((NB, 2 * NB), (0, 2 * NB), (0, NB))
    part_row, part_lane, inside = [], [], []
    for copy in early:
        copy.wait_recv()
    for e in range(3):
        partner = element + offs[e]
        part_row.append(partner >> 7)
        part_lane.append(partner & 127)
        if e == 0:
            kept = me > 0
        else:
            kept = (me < devices - e) | (partner < NB * BLK)
        inside.append(jnp.where(kept, 0.5, 0.0).astype(F32))
        begin, end = hot_rows[e]
        iota_row = lax.broadcasted_iota(jnp.int32, (end - begin, BLK), 0) + begin
        upright_lane = part_lane[e].astype(F32).T
        for k in range(NB):
            lane = pl.ds(k * BLK, BLK)
            lanes_hot[e, lane, :] = jnp.where(
                iota_lane == upright_lane[:, k : k + 1], 1.0, 0.0
            ).astype(BF16)
            rows_hot[hot_first[e] : hot_first[e] + end - begin, lane] = jnp.where(
                iota_row == part_row[e][k : k + 1], 1.0, 0.0
            ).astype(BF16)

    def gather(ref, e):
        out = []
        for v in range(NB // 8):
            lane = part_lane[e][8 * v : 8 * v + 8]
            hot = part_row[e][8 * v : 8 * v + 8]
            acc = jnp.zeros((8, BLK), F32)
            for h in range(max(8 * v, hot_rows[e][0]), 8 * v + 8 + NB):
                line = jnp.broadcast_to(ref[NB * e + h : NB * e + h + 1, :], (8, BLK))
                got = jnp.take_along_axis(line, lane, axis=1, mode="promise_in_bounds")
                acc = jnp.where(hot == h, got, acc)
            out.append(acc)
        return jnp.concatenate(out, 0)

    def scatter(flux, e):
        size = hot_rows[e][1] - hot_rows[e][0]
        hot_at = hot_first[e]
        at = 2 * hot_at
        top, rest = split(flux, 2)
        for k in range(NB):
            lane = pl.ds(k * BLK, BLK)
            hot = rows_hot[hot_at : hot_at + size, lane]
            for first_row, x in ((at, top), (at + size, rest)):
                line = jnp.broadcast_to(x[k : k + 1], (16, BLK)).astype(BF16)
                line = jnp.concatenate([line] * (size // 16), 0)
                spread[first_row : first_row + size, lane] = hot * line
        both = jnp.dot(spread[at : at + 2 * size, :], lanes_hot[e], preferred_element_type=F32)
        return both[:size] + both[size:]

    vecs = [table_inj[NB * e : NB * (e + 1), :] for e in range(3)]
    diffs = [vecs[e] - gather(table_inj, e) for e in range(3)]
    vec, sto = vecs[1], stores[0]

    def cubed(scale, t):
        aperture = scale * (1.0 + 0.5 * jnp.tanh(t))
        return aperture * aperture * aperture

    move0[3].wait_recv()
    move0[2].wait_recv()
    traction0 = first[NB:] + got_next[:NB, :]
    cubes = [
        cubed(bases[0], got_prev[...] + first[:NB]),
        cubed(bases[1], traction0),
    ]
    table[:NB, :] = cubes[0]
    table[NB : 2 * NB, :] = cubes[1]
    weights, fluxes, landed = [], [], []
    for e in range(3):
        if e == 1:
            move0[1].wait_recv()
            cubes.append(cubed(bases[2], got_next[NB:, :] + got_next2[:NB, :]))
            table[2 * NB : 3 * NB, :] = cubes[2]
        if e == 2:
            move0[0].wait_recv()
            table[3 * NB :, :] = cubed(bases[3], got_next2[NB:, :] + got_next3[...])
        weights.append(inside[e] * (cubes[e] + gather(table, e)))
        fluxes.append(weights[e] * diffs[e])
        landed.append(scatter(fluxes[e], e))
    weight = weights[1]
    q = sto * vec + fluxes[1] - landed[1][:NB] - landed[0]
    q_next = stores[1] * vecs[2] + fluxes[2] - landed[2] - landed[1][NB:]
    table[NB : 2 * NB, :] = q
    table[2 * NB : 3 * NB, :] = q_next
    q_diff = q - gather(table, 1)
    flux = weight * q_diff

    def line(x):
        return jnp.sum(x, axis=0, keepdims=True)

    rows = [line(vec * vec), line(vec * q), line(q * q), line(sto * q * q + flux * q_diff)]
    sums = jnp.concatenate(rows + [jnp.zeros((4, BLK), F32)], 0)

    def exchange(stage, sums, got):
        sums_out[stage] = sums
        for j in orders[stage]:
            pltpu.make_async_remote_copy(
                src_ref=sums_out.at[stage],
                dst_ref=got.at[j - 1],
                send_sem=red_send.at[stage],
                recv_sem=red_recv.at[stage],
                device_id=mate(stage, j),
                device_id_type=MESH,
            ).start()

    def collect(stage, sums, got):
        pltpu.make_async_copy(got, got, red_recv.at[stage]).wait()
        parts = [sums] + [got[j] for j in range(groups[stage] - 1)]
        while len(parts) > 1:
            parts = [sum(parts[j : j + 2]) for j in range(0, len(parts), 2)]
        return parts[0]

    exchange(0, sums, sums_near)
    landed = scatter(flux, 1)
    landed_out[...] = landed[NB:]
    move_u = send(landed_out, landed_in, 18, after)
    u_part = sto * q + flux - landed[:NB]
    sums = collect(0, sums, sums_near)
    exchange(1, sums, sums_far)
    move12.wait_recv()
    full = [
        traction0,
        others[NB:, :BLK] + got12[0],
        others[NB:, BLK:] + got12[1],
    ]
    for k in range(NB):
        rows = [x[k : k + 1] for x in full]
        traction[:, pl.ds(k * BLK, BLK)] = jnp.concatenate(rows, 0)
    move_u.wait_recv()
    u = u_part - landed_in[...]
    sums = collect(1, sums, sums_far)

    total = jnp.sum(sums, axis=1, keepdims=True)
    rr0, r0q, qq, qu = (total[j : j + 1] for j in range(4))
    alpha0 = rr0 / r0q
    rr1 = alpha0 * alpha0 * qq - rr0
    beta = rr1 / rr0
    alpha1 = rr1 / (r0q - 2.0 * alpha0 * qq + alpha0 * alpha0 * qu - beta * rr1 / alpha0)
    keep = 1.0 + beta
    r1 = vec - alpha0 * q
    residual[...] = r1 - alpha1 * (keep * q - alpha0 * u)
    pressure[...] = alpha0 * vec + alpha1 * (r1 + beta * vec)

    for copy in sum(frame, [frame_dsp]) + early + move0 + [move12, move_u]:
        copy.wait_send()
    pltpu.make_async_copy(sums_near, sums_near, red_send.at[0]).wait()
    pltpu.make_async_copy(sums_far, sums_far, red_send.at[1]).wait()


def deliver(traction_in, pressure_in, residual_in, traction, pressure, residual, sem):
    refs = ((traction_in, traction), (pressure_in, pressure), (residual_in, residual))
    copies = [pltpu.make_async_copy(a, b, sem.at[j]) for j, (a, b) in enumerate(refs)]
    for copy in copies:
        copy.start()
    for copy in copies:
        copy.wait()


def shards(
    grp_size,
    seg_size,
    positions,
    normals,
    scales,
    displacement,
    pair_list,
    pair_count,
    base_aperture,
    storage,
    injection,
    link_offset,
):
    low_size = 8 if seg_size % 8 == 0 else 2
    high_size = seg_size // low_size
    sizes = (grp_size // 2, 2, high_size, low_size)
    square = (NB, BLK)
    vmem = pl.BlockSpec(memory_space=pltpu.VMEM)
    anywhere = pl.BlockSpec(memory_space=pl.ANY)
    rows3 = pltpu.VMEM((3, NB * BLK), F32)
    tile = pltpu.VMEM(square, F32)
    double = pltpu.VMEM((2 * NB, BLK), F32)
    scratch = [
        rows3,
        rows3,
        tile,
        rows3,
        pltpu.SMEM((2, PMAX), jnp.int32),
        pltpu.VMEM((2, PMAX), jnp.int32),
        pltpu.SMEM((1,), jnp.int32),
        pltpu.VMEM((4, NB, BLK), F32),
        pltpu.VMEM((2, NB, BLK), F32),
        pltpu.VMEM((3, NB, BLK), jnp.int32),
        rows3,
        rows3,
        tile,
        rows3,
        pltpu.VMEM((4 * NB, BLK), F32),
        pltpu.VMEM((NB, BLK, 48), BF16),
        pltpu.VMEM((2 * NB, 48, 2 * BLK), BF16),
        pltpu.VMEM((2 * NB, 16, 2 * BLK), BF16),
        pltpu.VMEM((NB, 3, BLK, BLK), F32),
        pltpu.VMEM((UNROLL, BLK, 2 * BLK), BF16),
        pltpu.VMEM((3, PMAX // 8, 8, BLK), F32),
        pltpu.VMEM((3, PMAX // 8, 8, BLK), F32),
        double,
        pltpu.VMEM((2, NB, BLK), F32),
        tile,
        double,
        double,
        tile,
        pltpu.VMEM((2, NB, BLK), F32),
        pltpu.VMEM((2, 2 * NB, PMAX), BF16),
        pltpu.VMEM((3, NB * BLK, BLK), BF16),
        pltpu.VMEM((4 * NB, NB * BLK), BF16),
        pltpu.VMEM((8 * NB, NB * BLK), BF16),
        pltpu.VMEM((4 * NB, BLK), F32),
        tile,
        tile,
        pltpu.VMEM((2, 8, BLK), F32),
        pltpu.VMEM((2 * low_size - 1, 8, BLK), F32),
        pltpu.VMEM((grp_size // 2 * high_size - 1, 8, BLK), F32),
        pltpu.SemaphoreType.DMA((31,)),
        pltpu.SemaphoreType.DMA((31,)),
        pltpu.SemaphoreType.DMA((2,)),
        pltpu.SemaphoreType.DMA((2,)),
        pltpu.SemaphoreType.DMA((11,)),
    ]
    shapes = (
        jax.ShapeDtypeStruct((3, NB * BLK), F32),
        jax.ShapeDtypeStruct(square, F32),
        jax.ShapeDtypeStruct(square, F32),
    )
    outs = pl.pallas_call(
        functools.partial(kernel, sizes),
        out_shape=shapes,
        in_specs=[anywhere] * 10,
        out_specs=(vmem, vmem, vmem),
        scratch_shapes=scratch,
        compiler_params=pltpu.CompilerParams(
            collective_id=0, has_side_effects=True, vmem_limit_bytes=56 << 20
        ),
        name="network",
    )(
        positions,
        normals,
        scales.reshape(square),
        displacement,
        pair_list,
        pair_count,
        base_aperture.reshape(square),
        storage.reshape(square),
        injection.reshape(square),
        link_offset.reshape(square),
    )
    traction, pressure, residual = pl.pallas_call(
        deliver,
        out_shape=shapes,
        in_specs=[vmem] * 3,
        out_specs=(anywhere,) * 3,
        scratch_shapes=[pltpu.SemaphoreType.DMA((3,))],
        name="deliver",
    )(*outs)
    return traction, pressure.reshape(-1), residual.reshape(-1)


def solution(mesh):
    return jax.shard_map(
        functools.partial(shards, mesh.shape["grp"], mesh.shape["seg"]),
        mesh=mesh,
        in_specs=(
            P(None, ("grp", "seg")),
            P(None, ("grp", "seg")),
            P(("grp", "seg")),
            P(None, ("grp", "seg")),
            P(None, ("grp", "seg")),
            P(("grp", "seg")),
            P(("grp", "seg")),
            P(("grp", "seg")),
            P(("grp", "seg")),
            P(("grp", "seg")),
        ),
        out_specs=(P(None, ("grp", "seg")), P(("grp", "seg")), P(("grp", "seg"))),
        check_vma=False,
    )
```
